32 devices in a mesh: seq: 32 (over z, y, x, core).
Axes of the slice: x: 2, y: 2, z: 4, core: 2. Of those that a mesh axis runs over, the one named last changes fastest.
Arguments:
- queries: bfloat16 [8192, 8, 128], P('seq'), may hold values from -6 to 6
- key_rows: bfloat16 [8192, 4, 128], P('seq'), may hold values from -6 to 6
- value_rows: bfloat16 [8192, 4, 128], P('seq'), may hold values from -6 to 6
- attn_output: bfloat16 [8192, 8, 128], P('seq'), may hold values from -6 to 6
- grad_output: bfloat16 [8192, 8, 128], P('seq'), may hold values from -144 to 144
- log_norm: float32 [8, 8192], P(None, 'seq'), may hold values from 6.5 to 8
Outputs:
- grad_queries: bfloat16 [8192, 8, 128], P('seq')
- grad_keys: bfloat16 [8192, 4, 128], P('seq')
- grad_values: bfloat16 [8192, 4, 128], P('seq')
The draws below stay inside these ranges and needn't reach their ends.
All inputs are finite; a program needn't handle non-finite values.
Results may differ from the reference program's by a relative error of at most 0.0057.
Values may be sent and summed in bfloat16 or wider, within the bound.
No kernel may reach another device: no remote copies, remote signals or barrier semaphores. Data moves between devices by JAX's collectives and lax.ppermute only.
A program may use at most 64 MiB of HBM per device.

```python
import jax
import jax.numpy as jnp
from jax import lax

HD = 128
QH = 8
KVH = 4
W = 1024
TOK_DEV = 256
TOKENS = 8192


def levels(key, shape, split, low, largest):
    loudness = 1.0
    for position, parts in split:
        draws = jax.random.uniform(jax.random.fold_in(jax.random.fold_in(key, 6), position), (parts,), jnp.float32, low / len(split), largest / len(split))
        loudness = loudness * jnp.repeat(jnp.exp(draws), shape[position] // parts).reshape((-1,) + (1,) * (len(shape) - 1 - position))
    return loudness


def gaussian(rng, shape, width, reach, pieces=(), kind=jnp.bfloat16):
    entries = width * jax.random.normal(rng, shape, jnp.float32)
    if pieces:
        entries = entries * levels(rng, shape, pieces, -0.22, 0.18)
    return jnp.clip(entries, -reach, reach).astype(kind)


def setup_inputs(seed: int = 0) -> dict:
    key_of = jax.random.split(jax.random.key(seed), 7)
    queries = gaussian(key_of[0], (TOKENS, QH, HD), 1.0, 6.0, ((0, 32),))
    key_rows = gaussian(key_of[1], (TOKENS, KVH, HD), 1.0, 6.0, ((0, 32),))
    value_rows = gaussian(key_of[2], (TOKENS, KVH, HD), 1.0, 6.0, ((0, 32),))
    attn_output = gaussian(key_of[3], (TOKENS, QH, HD), 1.0, 6.0, ((0, 32),))
    grad_output = gaussian(key_of[4], (TOKENS, QH, HD), 24.0, 144.0, ((0, 32),))
    log_norm = jnp.clip(6.5 + 1.5 * jax.random.uniform(key_of[5], (QH, TOKENS), jnp.float32) ** levels(key_of[5], (QH, TOKENS), ((1, 32),), -0.2, 0.2), 6.5, 8.0)
    return dict(queries=queries, key_rows=key_rows, value_rows=value_rows, attn_output=attn_output, grad_output=grad_output, log_norm=log_norm)


query_scale = 168.0 ** -0.5


def band_mask(query_pos, key_pos, seq_rows):
    offset = query_pos[:, None] - key_pos[None, :]
    inside = (offset >= 0) & (offset < W)
    return inside & (key_pos >= 0)[None, :] & (query_pos < seq_rows)[:, None]


def band_grads(queries, grad_output, log_norm, delta_rows, key_rows, value_rows, allowed):
    row_count, head_count, head_size = queries.shape
    group_count = key_rows.shape[1]
    share = head_count // group_count
    query_group = queries.reshape(row_count, group_count, share, head_size).astype(jnp.float32)
    grad_group = grad_output.reshape(row_count, group_count, share, head_size).astype(jnp.float32)
    key_float = key_rows.astype(jnp.float32)
    value_float = value_rows.astype(jnp.float32)
    scores = jnp.einsum("qkgd,lkd->kgql", query_group, key_float) * query_scale
    norm_part = log_norm.reshape(group_count, share, row_count)[..., None]
    delta_part = delta_rows.reshape(group_count, share, row_count)[..., None]
    probs = jnp.where(allowed[None, None], jnp.exp(scores - norm_part), 0.0)
    probs_low = lax.optimization_barrier(probs.astype(jnp.bfloat16)).astype(jnp.float32)
    grad_v = jnp.einsum("kgql,qkgd->lkd", probs_low, grad_group)
    dprobs = jnp.einsum("qkgd,lkd->kgql", grad_group, value_float)
    dscores = lax.optimization_barrier((probs * (dprobs - delta_part)).astype(jnp.bfloat16)).astype(jnp.float32)
    grad_q = jnp.einsum("kgql,lkd->qkgd", dscores, key_float) * query_scale
    grad_k = jnp.einsum("kgql,qkgd->lkd", dscores, query_group) * query_scale
    return grad_q.reshape(row_count, head_count, head_size), grad_k, grad_v


def reference(queries, key_rows, value_rows, attn_output, grad_output, log_norm):
    total_rows = queries.shape[0]
    row_block = min(TOK_DEV, 128)
    hop_count = W // TOK_DEV
    front = jnp.zeros((W,) + key_rows.shape[1:], key_rows.dtype)
    padded_keys = jnp.concatenate([front, key_rows], 0)
    padded_values = jnp.concatenate([front, value_rows], 0)
    delta_rows = jnp.sum(grad_output.astype(jnp.float32) * attn_output.astype(jnp.float32), axis=-1).T
    distances = jnp.arange(hop_count + 1, dtype=jnp.int32)

    def visit(carry, block_index):
        total_k, total_v = carry
        start = (block_index * row_block).astype(jnp.int32)
        span = W + row_block
        query_pos = start + jnp.arange(row_block, dtype=jnp.int32)
        key_pos = start - W + jnp.arange(span, dtype=jnp.int32)
        allowed = band_mask(query_pos, key_pos, total_rows)
        grad_q, grad_k, grad_v = band_grads(
            lax.dynamic_slice_in_dim(queries, start, row_block, 0),
            lax.dynamic_slice_in_dim(grad_output, start, row_block, 0),
            lax.dynamic_slice_in_dim(log_norm, start, row_block, 1),
            lax.dynamic_slice_in_dim(delta_rows, start, row_block, 1),
            lax.dynamic_slice_in_dim(padded_keys, start, span, 0),
            lax.dynamic_slice_in_dim(padded_values, start, span, 0),
            allowed)
        query_dev = start // TOK_DEV
        key_dev = jnp.floor_divide(key_pos, TOK_DEV)
        apart = jnp.clip(query_dev - key_dev, 0, hop_count).astype(jnp.int32)
        picks = (apart[None, :] == distances[:, None]).astype(jnp.float32)[:, :, None, None]
        total_k = lax.dynamic_update_slice_in_dim(total_k, lax.dynamic_slice_in_dim(total_k, start, span, 1) + picks * grad_k[None], start, 1)
        total_v = lax.dynamic_update_slice_in_dim(total_v, lax.dynamic_slice_in_dim(total_v, start, span, 1) + picks * grad_v[None], start, 1)
        return (total_k, total_v), grad_q

    zeros_init = jnp.zeros((hop_count + 1, W + total_rows) + key_rows.shape[1:], jnp.float32)
    (total_k, total_v), grad_blocks = lax.scan(visit, (zeros_init, zeros_init), jnp.arange(total_rows // row_block, dtype=jnp.int32))
    grad_queries = grad_blocks.reshape(queries.shape).astype(jnp.bfloat16)
    far_k = lax.optimization_barrier(total_k[1:].astype(jnp.bfloat16)).astype(jnp.float32)
    far_v = lax.optimization_barrier(total_v[1:].astype(jnp.bfloat16)).astype(jnp.float32)
    own_k = total_k[0] + jnp.sum(far_k, axis=0)
    own_v = total_v[0] + jnp.sum(far_v, axis=0)
    return grad_queries, own_k[W:].astype(jnp.bfloat16), own_v[W:].astype(jnp.bfloat16)
```

```python
import functools
import math

import jax
import jax.numpy as jnp
from jax import lax
from jax.experimental import pallas as pl
from jax.experimental.pallas import tpu as pltpu
from jax.sharding import PartitionSpec as P

W = 1024

query_scale = 168.0 ** (-0.5)
LOG2E = math.log2(math.e)
AXIS = "seq"
VMEM_LIMIT = 48 * 1024 * 1024

NT = (((1,), (1,)), ((), ()))
NN = (((1,), (0,)), ((), ()))
TN = (((0,), (0,)), ((), ()))


def dot(a, b, dims):
    return lax.dot_general(a, b, dims, preferred_element_type=jnp.float32)


def call(kernel, name, out_shape, scratch=(), flops=0, aliases=None):
    return pl.pallas_call(
        kernel,
        out_shape=out_shape,
        scratch_shapes=list(scratch),
        name=name,
        input_output_aliases=aliases or {},
        cost_estimate=pl.CostEstimate(flops=flops, bytes_accessed=2 << 20, transcendentals=0),
        compiler_params=pltpu.CompilerParams(vmem_limit_bytes=VMEM_LIMIT),
    )


def pack_kv_kernel(k_ref, v_ref, keep_ref, give_ref, wide):
    rows, heads, _ = k_ref.shape
    half = heads // 2
    core = lax.axis_index(AXIS) % 2
    wide[:, :heads, :] = k_ref[...].astype(jnp.float32)
    wide[:, heads:, :] = v_ref[...].astype(jnp.float32)
    flat = wide.reshape(rows * 2 * heads, wide.shape[2])
    for out, side in ((keep_ref, core), (give_ref, 1 - core)):
        for part in range(2):
            for j in range(half):
                head = part * heads + side * half + j
                out[part * half + j] = flat[pl.ds(head, rows, stride=2 * heads), :].astype(out.dtype)


def pack_q_kernel(q_ref, g_ref, o_ref, norm_ref, keep_ref, give_ref, keep_rows, give_rows, wide):
    rows, heads, size = q_ref.shape
    half = heads // 2
    core = lax.axis_index(AXIS) % 2
    ones = jnp.ones((8, size), jnp.float32)
    flat = wide.reshape(rows * heads, size)
    sides = ((keep_ref, keep_rows, core), (give_ref, give_rows, 1 - core))
    wide[...] = q_ref[...].astype(jnp.float32)
    for out, _, side in sides:
        for j in range(half):
            out[j] = flat[pl.ds(side * half + j, rows, stride=heads), :].astype(out.dtype)
    wide[...] = g_ref[...].astype(jnp.float32)
    for out, _, side in sides:
        for j in range(half):
            out[half + j] = flat[pl.ds(side * half + j, rows, stride=heads), :].astype(out.dtype)
    wide[...] = g_ref[...].astype(jnp.float32) * o_ref[...].astype(jnp.float32)
    for _, out, side in sides:
        for j in range(half):
            product = flat[pl.ds(side * half + j, rows, stride=heads), :]
            total = lax.dot_general(
                ones, product, NT, precision=lax.Precision.HIGHEST, preferred_element_type=jnp.float32
            )
            out[j : j + 1] = norm_ref[pl.ds(side * half + j, 1), :] * LOG2E
            out[half + j : half + j + 1] = total[:1]


def tile(kv_ref, qg_ref, row_ref, grad_ref, gq_ref, offset, first):
    groups = kv_ref.shape[0] // 2
    share = qg_ref.shape[0] // (2 * groups)
    heads = groups * share
    rows, size = kv_ref.shape[1], kv_ref.shape[2]
    for g in range(groups):
        k = kv_ref[g]
        v = kv_ref[groups + g]
        q = qg_ref[g * share : (g + 1) * share].reshape(share * rows, size)
        d = qg_ref[heads + g * share : heads + (g + 1) * share].reshape(share * rows, size)
        norm = jnp.concatenate([row_ref[g * share + j : g * share + j + 1] for j in range(share)], 1)
        delta = jnp.concatenate([row_ref[heads + g * share + j : heads + g * share + j + 1] for j in range(share)], 1)
        x = dot(k, q, NT) * (query_scale * LOG2E) - norm
        if offset is not None:
            key = lax.broadcasted_iota(jnp.int32, (rows, rows), 0)
            query = lax.broadcasted_iota(jnp.int32, (rows, rows), 1)
            gap = query - key + offset
            seen = (gap >= 0) & (gap < W)
            x = jnp.concatenate(
                [jnp.where(seen, x[:, j * rows : (j + 1) * rows], -jnp.inf) for j in range(share)], 1
            )
        p = jnp.exp2(x)
        ds = (p * (dot(v, d, NT) - delta)).astype(jnp.bfloat16)
        gv = dot(p.astype(jnp.bfloat16), d, NN)
        gk = dot(ds, q, NN)
        gq = dot(ds, k, TN)
        if first:
            grad_ref[g] = gk
            grad_ref[groups + g] = gv
        else:
            grad_ref[g] += gk
            grad_ref[groups + g] += gv
        gq_ref[g] += gq


def scale_keys(grad_ref):
    groups = grad_ref.shape[0] // 2
    grad_ref[:groups] = grad_ref[:groups] * query_scale


def edge_kernel(back, kv_s, kv_r, qg_s, qg_r, rows_s, rows_r, gq_s_in, gq_r_in, grad_s, grad_r, gq_s, gq_r):
    device = lax.axis_index(AXIS)
    core = device % 2
    valid = device // 2 >= back
    rows = kv_s.shape[1]
    if back:
        gq_s[...] = gq_s_in[...]
        gq_r[...] = gq_r_in[...]
    else:
        gq_s[...] = jnp.zeros_like(gq_s)
        gq_r[...] = jnp.zeros_like(gq_r)

    @pl.when(valid)
    def _():
        tile(kv_s, qg_s, rows_s, grad_s, gq_s, 2 * back * rows, True)
        tile(kv_r, qg_r, rows_r, grad_r, gq_r, 2 * back * rows, True)
        full_from_s = (core == 0) if back == 0 else (core == 1)

        @pl.when(full_from_s)
        def _():
            tile(kv_s, qg_r, rows_r, grad_s, gq_r, None, False)

        @pl.when(jnp.logical_not(full_from_s))
        def _():
            tile(kv_r, qg_s, rows_s, grad_r, gq_s, None, False)

        scale_keys(grad_s)
        scale_keys(grad_r)

    if back:

        @pl.when(jnp.logical_not(valid))
        def _():
            grad_s[...] = jnp.zeros_like(grad_s)
            grad_r[...] = jnp.zeros_like(grad_r)


def full_kernel(kv, qg_s, qg_r, rows_s, rows_r, gq_s_in, gq_r_in, out, gq_s, gq_r, grad):
    valid = lax.axis_index(AXIS) // 2 >= 1
    gq_s[...] = gq_s_in[...]
    gq_r[...] = gq_r_in[...]

    @pl.when(valid)
    def _():
        tile(kv, qg_s, rows_s, grad, gq_s, None, True)
        tile(kv, qg_r, rows_r, grad, gq_r, None, False)
        scale_keys(grad)
        out[...] = grad[...].astype(out.dtype)

    @pl.when(jnp.logical_not(valid))
    def _():
        out[...] = jnp.zeros_like(out)


def final_q_kernel(own_ref, got_ref, out_ref, wide):
    rows, heads, size = out_ref.shape
    half = heads // 2
    core = lax.axis_index(AXIS) % 2
    flat = wide.reshape(rows * heads, size)
    groups = own_ref.shape[0]
    share = half // groups
    for j in range(half):
        g, r = j // share, j % share
        flat[pl.ds(core * half + j, rows, stride=heads), :] = own_ref[g, r * rows : (r + 1) * rows] * query_scale
        flat[pl.ds((1 - core) * half + j, rows, stride=heads), :] = got_ref[g, r * rows : (r + 1) * rows].astype(
            jnp.float32
        )
    out_ref[...] = wide[...].astype(out_ref.dtype)


def final_kv_kernel(own_ref, got_ref, back_s, back_r, side_s, side_r, out_k, out_v, wide):
    rows, heads, size = out_k.shape
    half = heads // 2
    device = lax.axis_index(AXIS)
    core = device % 2
    even = jnp.where((device // 2) % 2 == 0, 1.0, 0.0).astype(jnp.float32)
    flat = wide.reshape(rows * 2 * heads, size)
    for side, base_ref, back_ref, near_ref in (
        (core, own_ref, back_s, side_s),
        (1 - core, got_ref, back_r, side_r),
    ):
        for part in range(2):
            for j in range(half):
                n = part * half + j
                total = (
                    base_ref[n].astype(jnp.float32)
                    + back_ref[n].astype(jnp.float32)
                    + near_ref[n].astype(jnp.float32) * even
                )
                flat[pl.ds(part * heads + side * half + j, rows, stride=2 * heads), :] = total
    out_k[...] = wide[:, :heads, :].astype(out_k.dtype)
    out_v[...] = wide[:, heads:, :].astype(out_v.dtype)


def shards(queries, key_rows, value_rows, attn_output, grad_output, log_norm):
    rows, heads, size = queries.shape
    groups = key_rows.shape[1]
    devices = lax.axis_size(AXIS)
    hops = W // rows
    assert hops == 4 and devices % 4 == 0
    low, f32 = jnp.bfloat16, jnp.float32
    device = lax.axis_index(AXIS)
    even = (device // 2) % 2 == 0

    def move(x, target):
        return lax.ppermute(x, AXIS, [(i, target(i)) for i in range(devices)])

    ahead = lambda i: (i + hops) % devices
    behind = lambda i: (i - hops) % devices
    sibling = lambda i: i ^ 1
    beside = lambda i: i ^ 2

    shape = jax.ShapeDtypeStruct
    kv_block = (groups, rows, size)
    qg_block = (heads, rows, size)
    row_block = (heads, rows)
    gq_block = (groups // 2, heads // groups * rows, size)
    tile_flops = 10 * rows * rows * size * heads // 2

    kv_s, kv_give = call(
        pack_kv_kernel,
        "pack_kv",
        [shape(kv_block, low)] * 2,
        [pltpu.VMEM((rows, 2 * groups, size), f32)],
    )(key_rows, value_rows)
    two_s = move(kv_s, ahead)
    kv_r = move(kv_give, sibling)
    two_r = move(kv_r, ahead)
    qg_s, qg_give, rows_s, rows_give = call(
        pack_q_kernel,
        "pack_q",
        [shape(qg_block, low)] * 2 + [shape(row_block, f32)] * 2,
        [pltpu.VMEM((rows, heads, size), f32)],
    )(queries, grad_output, attn_output, log_norm)
    qg_r = move(qg_give, sibling)
    rows_r = move(rows_give, sibling)
    one_s = move(jnp.where(even, kv_s, two_s), beside)
    one_r = move(jnp.where(even, kv_r, two_r), beside)

    def edge(back, block_s, block_r, gq_s, gq_r):
        return call(
            functools.partial(edge_kernel, back),
            "edge%d" % back,
            [shape(kv_block, f32)] * 2 + [shape(gq_block, f32)] * 2,
            flops=3 * tile_flops,
            aliases={6: 2, 7: 3},
        )(block_s, block_r, qg_s, qg_r, rows_s, rows_r, gq_s, gq_r)

    def full(block, gq_s, gq_r):
        return call(
            full_kernel,
            "full",
            [shape(kv_block, low)] + [shape(gq_block, f32)] * 2,
            [pltpu.VMEM(kv_block, f32)],
            flops=2 * tile_flops,
            aliases={5: 1, 6: 2},
        )(block, qg_s, qg_r, rows_s, rows_r, gq_s, gq_r)

    zero = jnp.zeros(gq_block, f32)
    own_s, own_r, gq_s, gq_r = edge(0, kv_s, kv_r, zero, zero)
    local_r = move(own_r.astype(low), sibling)
    far_s, far_r, gq_s, gq_r = edge(2, two_s, two_r, gq_s, gq_r)
    near_s, gq_s, gq_r = full(one_s, gq_s, gq_r)
    side_s = move(near_s, beside)
    near_r, gq_s, gq_r = full(one_r, gq_s, gq_r)
    side_r = move(near_r, lambda i: i ^ 3 if i & 2 else i ^ 2)

    def join(far, side):
        return (far + jnp.where(even, 0.0, side.astype(f32))).astype(low)

    back_s = move(join(far_s, side_s), behind)
    back_r = move(join(far_r, side_r), lambda i: sibling(behind(i)))
    gq_got = move((gq_r * query_scale).astype(low), sibling)
    grad_q = call(
        final_q_kernel,
        "final_q",
        shape(queries.shape, low),
        [pltpu.VMEM((rows, heads, size), f32)],
    )(gq_s, gq_got)
    grad_k, grad_v = call(
        final_kv_kernel,
        "final_kv",
        [shape(key_rows.shape, low), shape(value_rows.shape, low)],
        [pltpu.VMEM((rows, 2 * groups, size), f32)],
    )(own_s, local_r, back_s, back_r, side_s, side_r)
    return grad_q, grad_k, grad_v


def solution(mesh):
    in_specs = (
        P("seq", None, None),
        P("seq", None, None),
        P("seq", None, None),
        P("seq", None, None),
        P("seq", None, None),
        P(None, "seq"),
    )
    out_specs = (P("seq", None, None), P("seq", None, None), P("seq", None, None))
    return jax.shard_map(shards, mesh=mesh, in_specs=in_specs, out_specs=out_specs, check_vma=False)
```

```python
import functools
import math

import jax
import jax.numpy as jnp
from jax import lax
from jax.experimental import pallas as pl
from jax.experimental.pallas import tpu as pltpu
from jax.sharding import PartitionSpec as P

W = 1024

query_scale = 168.0 ** (-0.5)
LOG2E = math.log2(math.e)
AXIS = "seq"
VMEM_LIMIT = 48 * 1024 * 1024

NT = (((1,), (1,)), ((), ()))
NN = (((1,), (0,)), ((), ()))
TN = (((0,), (0,)), ((), ()))


def dot(a, b, dims):
    return lax.dot_general(a, b, dims, preferred_element_type=jnp.float32)


def call(kernel, name, out_shape, scratch=(), flops=0, in_specs=None):
    specs = {} if in_specs is None else {"in_specs": in_specs}
    return pl.pallas_call(
        kernel,
        out_shape=out_shape,
        scratch_shapes=list(scratch),
        name=name,
        cost_estimate=pl.CostEstimate(flops=flops, bytes_accessed=2 << 20, transcendentals=0),
        compiler_params=pltpu.CompilerParams(vmem_limit_bytes=VMEM_LIMIT),
        **specs,
    )


def fetch(pairs, sems):
    copies = [pltpu.make_async_copy(src, dst, sems.at[n]) for n, (src, dst) in enumerate(pairs)]
    for copy in copies:
        copy.start()
    return copies


def pack_kv_kernel(k_hbm, v_hbm, keep_ref, give_ref, k_ref, v_ref, wide, sems):
    copy_k, copy_v = fetch(((k_hbm, k_ref), (v_hbm, v_ref)), sems)
    rows, heads, _ = k_ref.shape
    half = heads // 2
    core = lax.axis_index(AXIS) % 2
    copy_k.wait()
    wide[:, :heads, :] = k_ref[...].astype(jnp.float32)
    copy_v.wait()
    wide[:, heads:, :] = v_ref[...].astype(jnp.float32)
    flat = wide.reshape(rows * 2 * heads, wide.shape[2])
    for out, side in ((keep_ref, core), (give_ref, 1 - core)):
        for part in range(2):
            for j in range(half):
                head = part * heads + side * half + j
                out[part * half + j] = flat[pl.ds(head, rows, stride=2 * heads), :].astype(out.dtype)


def split_three(x):
    parts = []
    for _ in range(3):
        part = x.astype(jnp.bfloat16)
        parts.append(part)
        x = x - part.astype(jnp.float32)
    return parts


def join_three(ref, start, count):
    high, mid, low = (ref[start + n * count : start + (n + 1) * count].astype(jnp.float32) for n in range(3))
    return high + mid + low


def pack_q_kernel(
    q_hbm, g_hbm, o_hbm, norm_ref, after, keep_ref, keep_rows, give_ref, q_ref, g_ref, o_ref, wide, give_rows, sems
):
    copy_q, copy_g, copy_o = fetch(((q_hbm, q_ref), (g_hbm, g_ref), (o_hbm, o_ref)), sems)
    rows, heads, size = q_ref.shape
    half = heads // 2
    pieces = rows // size
    core = lax.axis_index(AXIS) % 2
    ones = jnp.ones((8, size), jnp.float32)
    flat = wide.reshape(rows * heads, size)
    sides = ((keep_ref, keep_rows, core), (give_ref, give_rows, 1 - core))

    def spread(base):
        for out, _, side in sides:
            for j in range(half):
                block = flat[pl.ds(side * half + j, rows, stride=heads), :]
                out[(base + j) * rows : (base + j + 1) * rows] = block.astype(out.dtype)

    copy_q.wait()
    wide[...] = q_ref[...].astype(jnp.float32)
    spread(0)
    copy_g.wait()
    wide[...] = g_ref[...].astype(jnp.float32)
    spread(half)
    copy_o.wait()
    wide[...] = g_ref[...].astype(jnp.float32) * o_ref[...].astype(jnp.float32)
    for _, out, side in sides:
        for j in range(half):
            product = flat[pl.ds(side * half + j, rows, stride=heads), :]
            delta = lax.dot_general(
                ones, product, NT, precision=lax.Precision.HIGHEST, preferred_element_type=jnp.float32
            )
            norm = norm_ref[pl.ds(side * half + j, 1), :] * LOG2E
            for n in range(pieces):
                out[j * pieces + n : j * pieces + n + 1] = norm[:, n * size : (n + 1) * size]
                at = (half + j) * pieces + n
                out[at : at + 1] = delta[:1, n * size : (n + 1) * size]
    count = heads * pieces
    for n, part in enumerate(split_three(give_rows[...])):
        give_ref[heads * rows + n * count : heads * rows + (n + 1) * count] = part


def rows_of(row_ref, qg_ref, rows, size):
    if row_ref is not None:
        return row_ref[...]
    total = qg_ref.shape[0] - qg_ref.shape[0] % rows
    return join_three(qg_ref, total, (qg_ref.shape[0] - total) // 3)


def tile(kv_ref, side, grad_ref, gq_in, gq_ref, offset, first):
    qg_ref, row_ref = side
    groups = kv_ref.shape[0] // 2
    rows, size = kv_ref.shape[1], kv_ref.shape[2]
    span = gq_ref.shape[1]
    share = span // rows
    heads = groups * share
    pieces = span // size
    vectors = rows_of(row_ref, qg_ref, rows, size)

    def vector(at):
        return jnp.concatenate([vectors[at + n : at + n + 1] for n in range(pieces)], 1)

    for g in range(groups):
        k = kv_ref[g]
        v = kv_ref[groups + g]
        q = qg_ref[g * span : (g + 1) * span]
        d = qg_ref[heads * rows + g * span : heads * rows + (g + 1) * span]
        norm = vector(g * pieces)
        delta = vector((groups + g) * pieces)
        x = dot(k, q, NT) * (query_scale * LOG2E) - norm
        if offset is not None:
            key = lax.broadcasted_iota(jnp.int32, (rows, rows), 0)
            query = lax.broadcasted_iota(jnp.int32, (rows, rows), 1)
            gap = query - key + offset
            seen = (gap >= 0) & (gap < W)
            x = jnp.concatenate(
                [jnp.where(seen, x[:, j * rows : (j + 1) * rows], -jnp.inf) for j in range(share)], 1
            )
        p = jnp.exp2(x)
        ds = (p * (dot(v, d, NT) - delta)).astype(jnp.bfloat16)
        gv = dot(p.astype(jnp.bfloat16), d, NN)
        gk = dot(ds, q, NN)
        gq = dot(ds, k, TN)
        if first:
            grad_ref[g] = gk
            grad_ref[groups + g] = gv
        else:
            grad_ref[g] += gk
            grad_ref[groups + g] += gv
        gq_ref[g] = gq if gq_in is None else gq_in[g] + gq


def scale_keys(grad_ref):
    groups = grad_ref.shape[0] // 2
    grad_ref[:groups] = grad_ref[:groups] * query_scale


def own_kernel(kv_s, kv_r, qg_s, rows_s, qg_r, gq_s_in, gq_r_in, grad_s, grad_r, gq_s, gq_r):
    side_s, side_r = (qg_s, rows_s), (qg_r, None)
    core = lax.axis_index(AXIS) % 2
    tile(kv_s, side_s, grad_s, gq_s_in, gq_s, 0, True)
    tile(kv_r, side_r, grad_r, gq_r_in, gq_r, 0, True)

    @pl.when(core == 0)
    def _():
        tile(kv_s, side_r, grad_s, gq_r, gq_r, None, False)

    @pl.when(core == 1)
    def _():
        tile(kv_r, side_s, grad_r, gq_s, gq_s, None, False)

    scale_keys(grad_s)
    scale_keys(grad_r)


def far_kernel(first, kv, qg_s, rows_s, qg_r, *refs):
    if first:
        out, gq_s, gq_r, grad = refs
        side_s, side_r, seen_by = (qg_s, rows_s), (qg_r, None), 1
    else:
        gq_r_in, gq_s_in, out, gq_r, gq_s, grad = refs
        side_s, side_r, seen_by = (qg_r, None), (qg_s, rows_s), 0
    device = lax.axis_index(AXIS)
    core = device % 2
    valid = device // 2 >= 2
    rows = kv.shape[1]

    @pl.when(valid)
    def _():
        tile(kv, side_s, grad, None if first else gq_s_in, gq_s, W, True)

    @pl.when(valid & (core == seen_by))
    def _():
        tile(kv, side_r, grad, None if first else gq_r_in, gq_r, None, False)

    @pl.when(valid)
    def _():
        scale_keys(grad)
        out[...] = grad[...].astype(out.dtype)

    @pl.when(jnp.logical_not(valid))
    def _():
        out[...] = jnp.zeros_like(out)
        gq_s[...] = jnp.zeros_like(gq_s) if first else gq_s_in[...]

    @pl.when(jnp.logical_not(valid & (core == seen_by)))
    def _():
        gq_r[...] = jnp.zeros_like(gq_r) if first else gq_r_in[...]


def near_kernel(kv, qg_s, rows_s, qg_r, gq_s_in, gq_r_in, out, gq_s, gq_r, grad):
    side_s, side_r = (qg_s, rows_s), (qg_r, None)
    valid = lax.axis_index(AXIS) // 2 >= 1

    @pl.when(valid)
    def _():
        tile(kv, side_s, grad, gq_s_in, gq_s, None, True)
        tile(kv, side_r, grad, gq_r_in, gq_r, None, False)
        scale_keys(grad)
        out[...] = grad[...].astype(out.dtype)

    @pl.when(jnp.logical_not(valid))
    def _():
        out[...] = jnp.zeros_like(out)
        gq_s[...] = gq_s_in[...]
        gq_r[...] = gq_r_in[...]


def final_q_kernel(own_ref, got_ref, out_ref, wide):
    rows, heads, size = out_ref.shape
    half = heads // 2
    core = lax.axis_index(AXIS) % 2
    flat = wide.reshape(rows * heads, size)
    share = half // own_ref.shape[0]
    skip = got_ref.shape[0] - half
    for j in range(half):
        g, r = j // share, j % share
        flat[pl.ds(core * half + j, rows, stride=heads), :] = own_ref[g, r * rows : (r + 1) * rows] * query_scale
        flat[pl.ds((1 - core) * half + j, rows, stride=heads), :] = got_ref[skip + j].astype(jnp.float32)
    out_ref[...] = wide[...].astype(out_ref.dtype)


def final_kv_kernel(own_ref, got_ref, back_s, back_r, side_s, side_r, out_k, out_v, wide):
    rows, heads, size = out_k.shape
    half = heads // 2
    device = lax.axis_index(AXIS)
    core = device % 2
    even = jnp.where((device // 2) % 2 == 0, 1.0, 0.0).astype(jnp.float32)
    flat = wide.reshape(rows * 2 * heads, size)
    for side, base_ref, back_ref, near_ref, share in (
        (core, own_ref, back_s, side_s, None),
        (1 - core, got_ref, back_r, side_r, even),
    ):
        for part in range(2):
            for j in range(half):
                n = part * half + j
                near = near_ref[n].astype(jnp.float32)
                near = near if share is None else near * share
                total = base_ref[n].astype(jnp.float32) + back_ref[n].astype(jnp.float32) + near
                flat[pl.ds(part * heads + side * half + j, rows, stride=2 * heads), :] = total
    out_k[...] = wide[:, :heads, :].astype(out_k.dtype)
    out_v[...] = wide[:, heads:, :].astype(out_v.dtype)


def shards(queries, key_rows, value_rows, attn_output, grad_output, log_norm):
    rows, heads, size = queries.shape
    groups = key_rows.shape[1]
    devices = lax.axis_size(AXIS)
    hops = W // rows
    assert hops == 4 and devices % 4 == 0
    low, f32 = jnp.bfloat16, jnp.float32
    device = lax.axis_index(AXIS)
    even = (device // 2) % 2 == 0

    def move(x, target):
        return lax.ppermute(x, AXIS, [(i, target(i)) for i in range(devices)])

    ahead = lambda i: (i + hops) % devices
    behind = lambda i: (i - hops) % devices
    sibling = lambda i: i ^ 1
    beside = lambda i: i ^ 2

    shape = jax.ShapeDtypeStruct
    kv_block = (groups, rows, size)
    qg_rows = heads * rows
    row_block = (heads * rows // size, size)
    gq_block = (groups // 2, heads // groups * rows, size)
    tile_flops = 10 * rows * rows * size * heads // 2

    hbm = pl.BlockSpec(memory_space=pltpu.HBM)
    vmem = pl.BlockSpec(memory_space=pltpu.VMEM)
    anywhere = pl.BlockSpec(memory_space=pl.ANY)
    hbm = pl.BlockSpec(memory_space=pltpu.HBM)
    vmem = pl.BlockSpec(memory_space=pltpu.VMEM)
    anywhere = pl.BlockSpec(memory_space=pl.ANY)

    def pin(x):
        return pltpu.with_memory_space_constraint(x, pltpu.HBM)

    kv_s, kv_give = call(
        pack_kv_kernel,
        "pack_kv",
        [shape(kv_block, low)] * 2,
        [pltpu.VMEM(key_rows.shape, low)] * 2
        + [pltpu.VMEM((rows, 2 * groups, size), f32), pltpu.SemaphoreType.DMA((2,))],
        in_specs=[hbm, hbm],
    )(pin(key_rows), pin(value_rows))
    kv_r = move(kv_give, sibling)
    two_s = move(kv_s, ahead)
    one_r = move(kv_r, lambda i: (i + 2) % devices)
    two_r = move(kv_r, ahead)
    qg_s, rows_s, qg_give = call(
        pack_q_kernel,
        "pack_q",
        [shape((qg_rows, size), low), shape(row_block, f32), shape((qg_rows + 3 * row_block[0], size), low)],
        [pltpu.VMEM(queries.shape, low)] * 3
        + [pltpu.VMEM((rows, heads, size), f32), pltpu.VMEM(row_block, f32), pltpu.SemaphoreType.DMA((3,))],
        in_specs=[hbm, hbm, hbm, vmem, anywhere],
    )(pin(queries), pin(grad_output), pin(attn_output), log_norm, kv_r)
    qg_r = move(qg_give, sibling)
    one_s = move(jnp.where(even, kv_s, two_s), beside)

    acc = [shape(gq_block, f32)] * 2
    grad_scratch = [pltpu.VMEM(kv_block, f32)]
    sides = (qg_s, rows_s, qg_r)
    far_s, gq_s, gq_r = call(
        functools.partial(far_kernel, True),
        "far_s",
        [shape(kv_block, low)] + acc,
        grad_scratch,
        flops=2 * tile_flops,
    )(two_s, *sides)
    back_s = move(far_s, behind)
    own_s, own_r, gq_s, gq_r = call(
        own_kernel, "own", [shape(kv_block, f32)] * 2 + acc, flops=3 * tile_flops
    )(kv_s, kv_r, *sides, gq_s, gq_r)
    near = functools.partial(
        call, near_kernel, out_shape=[shape(kv_block, low)] + acc, scratch=grad_scratch, flops=2 * tile_flops
    )
    near_r, gq_s, gq_r = near(name="near_r")(one_r, *sides, gq_s, gq_r)
    side_r = move(near_r, lambda i: i ^ 3 if i & 2 else i ^ 2)
    near_s, gq_s, gq_r = near(name="near_s")(one_s, *sides, gq_s, gq_r)
    side_s = move(near_s, lambda i: (i - 2) % devices)
    far_r, gq_s, gq_r = call(
        functools.partial(far_kernel, False),
        "far_r",
        [shape(kv_block, f32)] + acc,
        grad_scratch,
        flops=2 * tile_flops,
    )(two_r, *sides, gq_s, gq_r)
    side_r, back_s = lax.optimization_barrier((side_r, back_s))
    joined = (far_r + jnp.where(even, 0.0, side_r.astype(f32))).astype(low)
    back_r = move(joined, lambda i: sibling(behind(i)))
    give = jnp.concatenate([own_r.astype(low), (gq_r * query_scale).astype(low).reshape(-1, rows, size)])
    got = move(give, sibling)
    grad_q = call(
        final_q_kernel,
        "final_q",
        shape(queries.shape, low),
        [pltpu.VMEM((rows, heads, size), f32)],
    )(gq_s, got)
    grad_k, grad_v = call(
        final_kv_kernel,
        "final_kv",
        [shape(key_rows.shape, low), shape(value_rows.shape, low)],
        [pltpu.VMEM((rows, 2 * groups, size), f32)],
    )(own_s, got, back_s, back_r, side_s, side_r)
    return grad_q, grad_k, grad_v


def solution(mesh):
    in_specs = (
        P("seq", None, None),
        P("seq", None, None),
        P("seq", None, None),
        P("seq", None, None),
        P("seq", None, None),
        P(None, "seq"),
    )
    out_specs = (P("seq", None, None), P("seq", None, None), P("seq", None, None))
    return jax.shard_map(shards, mesh=mesh, in_specs=in_specs, out_specs=out_specs, check_vma=False)
```

```python
import functools
import math

import jax
import jax.numpy as jnp
from jax import lax
from jax.experimental import pallas as pl
from jax.experimental.pallas import tpu as pltpu
from jax.sharding import PartitionSpec as P

W = 1024

query_scale = 168.0 ** (-0.5)
LOG2E = math.log2(math.e)
AXIS = "seq"
VMEM_LIMIT = 16 * 1024 * 1024
LONG = 10**9

NT = (((1,), (1,)), ((), ()))
NN = (((1,), (0,)), ((), ()))
TN = (((0,), (0,)), ((), ()))


def dot(a, b, dims):
    return lax.dot_general(a, b, dims, preferred_element_type=jnp.float32)


def call(kernel, name, out_shape, scratch=(), flops=0, in_specs=None):
    specs = {} if in_specs is None else {"in_specs": in_specs}
    return pl.pallas_call(
        kernel,
        out_shape=out_shape,
        scratch_shapes=list(scratch),
        name=name,
        cost_estimate=pl.CostEstimate(flops=flops, bytes_accessed=2 << 20, transcendentals=0),
        compiler_params=pltpu.CompilerParams(vmem_limit_bytes=VMEM_LIMIT),
        **specs,
    )


def fetch(pairs, sems):
    copies = [pltpu.make_async_copy(src, dst, sems.at[n]) for n, (src, dst) in enumerate(pairs)]
    for copy in copies:
        copy.start()
    return copies


def pack_kv_kernel(k_hbm, v_hbm, keep_ref, give_ref, k_ref, v_ref, wide, sems):
    copy_k, copy_v = fetch(((k_hbm, k_ref), (v_hbm, v_ref)), sems)
    rows, heads, _ = k_ref.shape
    half = heads // 2
    core = lax.axis_index(AXIS) % 2
    copy_k.wait()
    wide[:, :heads, :] = k_ref[...].astype(jnp.float32)
    copy_v.wait()
    wide[:, heads:, :] = v_ref[...].astype(jnp.float32)
    flat = wide.reshape(rows * 2 * heads, wide.shape[2])
    for out, side in ((keep_ref, core), (give_ref, 1 - core)):
        for part in range(2):
            for j in range(half):
                head = part * heads + side * half + j
                out[part * half + j] = flat[pl.ds(head, rows, stride=2 * heads), :].astype(out.dtype)


def split_three(x):
    parts = []
    for _ in range(3):
        part = x.astype(jnp.bfloat16)
        parts.append(part)
        x = x - part.astype(jnp.float32)
    return parts


def join_three(ref, start, count):
    high, mid, low = (ref[start + n * count : start + (n + 1) * count].astype(jnp.float32) for n in range(3))
    return high + mid + low


def pack_q_kernel(
    q_hbm,
    g_hbm,
    o_hbm,
    norm_ref,
    after,
    keep_q,
    keep_g,
    keep_rows,
    give_q,
    give_g,
    q_ref,
    g_ref,
    o_ref,
    wide,
    give_rows,
    sems,
):
    copy_q, copy_g, copy_o = fetch(((q_hbm, q_ref), (g_hbm, g_ref), (o_hbm, o_ref)), sems)
    rows, heads, size = q_ref.shape
    half = heads // 2
    pieces = rows // size
    core = lax.axis_index(AXIS) % 2
    ones = jnp.ones((8, size), jnp.float32)
    flat = wide.reshape(rows * heads, size)

    def spread(outs):
        for out, side in zip(outs, (core, 1 - core), strict=True):
            for j in range(half):
                block = flat[pl.ds(side * half + j, rows, stride=heads), :]
                out[j * rows : (j + 1) * rows] = block.astype(out.dtype)

    copy_q.wait()
    wide[...] = q_ref[...].astype(jnp.float32)
    spread((keep_q, give_q))
    copy_g.wait()
    wide[...] = g_ref[...].astype(jnp.float32)
    spread((keep_g, give_g))
    copy_o.wait()
    wide[...] = g_ref[...].astype(jnp.float32) * o_ref[...].astype(jnp.float32)
    for out, side in ((keep_rows, core), (give_rows, 1 - core)):
        for j in range(half):
            product = flat[pl.ds(side * half + j, rows, stride=heads), :]
            delta = lax.dot_general(
                ones, product, NT, precision=lax.Precision.HIGHEST, preferred_element_type=jnp.float32
            )
            norm = norm_ref[pl.ds(side * half + j, 1), :] * LOG2E
            for n in range(pieces):
                out[j * pieces + n : j * pieces + n + 1] = norm[:, n * size : (n + 1) * size]
                at = (half + j) * pieces + n
                out[at : at + 1] = delta[:1, n * size : (n + 1) * size]
    count = heads * pieces
    for n, part in enumerate(split_three(give_rows[...])):
        give_q[half * rows + n * count : half * rows + (n + 1) * count] = part


def tile(kv_ref, side, grad_ref, gq_in, gq_ref, offset, first):
    q_ref, g_ref, row_ref = side
    groups = kv_ref.shape[0] // 2
    rows, size = kv_ref.shape[1], kv_ref.shape[2]
    span = gq_ref.shape[1]
    share = span // rows
    pieces = span // size
    if row_ref is None:
        vectors = join_three(q_ref, g_ref.shape[0], 2 * groups * pieces)
    else:
        vectors = row_ref[...]

    def vector(at):
        return jnp.concatenate([vectors[at + n : at + n + 1] for n in range(pieces)], 1)

    for g in range(groups):
        k = kv_ref[g]
        v = kv_ref[groups + g]
        q = q_ref[g * span : (g + 1) * span]
        d = g_ref[g * span : (g + 1) * span]
        norm = vector(g * pieces)
        delta = vector((groups + g) * pieces)
        x = dot(k, q, NT) * (query_scale * LOG2E) - norm
        if offset is not None:
            key = lax.broadcasted_iota(jnp.int32, (rows, rows), 0)
            query = lax.broadcasted_iota(jnp.int32, (rows, rows), 1)
            gap = query - key + offset
            seen = (gap >= 0) & (gap < W)
            x = jnp.concatenate(
                [jnp.where(seen, x[:, j * rows : (j + 1) * rows], -jnp.inf) for j in range(share)], 1
            )
        p = jnp.exp2(x)
        ds = (p * (dot(v, d, NT) - delta)).astype(jnp.bfloat16)
        gv = dot(p.astype(jnp.bfloat16), d, NN)
        gk = dot(ds, q, NN)
        gq = dot(ds, k, TN)
        if first:
            grad_ref[g] = gk
            grad_ref[groups + g] = gv
        else:
            grad_ref[g] += gk
            grad_ref[groups + g] += gv
        gq_ref[g] = gq if gq_in is None else gq_in[g] + gq


def scale_keys(grad_ref):
    groups = grad_ref.shape[0] // 2
    grad_ref[:groups] = grad_ref[:groups] * query_scale


def own_side_kernel(kv_s, q_s, g_s, rows_s, grad_s, gq_s):
    tile(kv_s, (q_s, g_s, rows_s), grad_s, None, gq_s, 0, True)


def own_rest_kernel(kv_s, kv_r, q_s, g_s, rows_s, q_r, g_r, grad_s_in, gq_s_in, gq_r_in, grad_s, grad_r, gq_s, gq_r):
    side_s, side_r = (q_s, g_s, rows_s), (q_r, g_r, None)
    core = lax.axis_index(AXIS) % 2
    grad_s[...] = grad_s_in[...]
    tile(kv_r, side_r, grad_r, gq_r_in, gq_r, 0, True)

    @pl.when(core == 0)
    def _():
        tile(kv_s, side_r, grad_s, gq_r, gq_r, None, False)
        gq_s[...] = gq_s_in[...]

    @pl.when(core == 1)
    def _():
        tile(kv_r, side_s, grad_r, gq_s_in, gq_s, None, False)

    scale_keys(grad_s)
    scale_keys(grad_r)


def far_kernel(first, kv, q_s, g_s, rows_s, q_r, g_r, *refs):
    if first:
        gq_s_in, out, gq_s, gq_r, grad = refs
        gq_r_in, side_s, side_r, seen_by = None, (q_s, g_s, rows_s), (q_r, g_r, None), 1
    else:
        gq_r_in, gq_s_in, out, gq_r, gq_s, grad = refs
        side_s, side_r, seen_by = (q_r, g_r, None), (q_s, g_s, rows_s), 0
    device = lax.axis_index(AXIS)
    core = device % 2
    valid = device // 2 >= 2

    @pl.when(valid)
    def _():
        tile(kv, side_s, grad, gq_s_in, gq_s, W, True)

    @pl.when(valid & (core == seen_by))
    def _():
        tile(kv, side_r, grad, gq_r_in, gq_r, None, False)

    @pl.when(valid)
    def _():
        scale_keys(grad)
        out[...] = grad[...].astype(out.dtype)

    @pl.when(jnp.logical_not(valid))
    def _():
        out[...] = jnp.zeros_like(out)
        gq_s[...] = gq_s_in[...]

    @pl.when(jnp.logical_not(valid & (core == seen_by)))
    def _():
        gq_r[...] = jnp.zeros_like(gq_r) if first else gq_r_in[...]


def near_kernel(kv, q_s, g_s, rows_s, q_r, g_r, gq_s_in, gq_r_in, out, gq_s, gq_r, grad):
    side_s, side_r = (q_s, g_s, rows_s), (q_r, g_r, None)
    valid = lax.axis_index(AXIS) // 2 >= 1

    @pl.when(valid)
    def _():
        tile(kv, side_s, grad, gq_s_in, gq_s, None, True)
        tile(kv, side_r, grad, gq_r_in, gq_r, None, False)
        scale_keys(grad)
        out[...] = grad[...].astype(out.dtype)

    @pl.when(jnp.logical_not(valid))
    def _():
        out[...] = jnp.zeros_like(out)
        gq_s[...] = gq_s_in[...]
        gq_r[...] = gq_r_in[...]


def final_q_kernel(own_ref, got_ref, out_ref, token_ref, wide):
    token_ref[...] = jnp.zeros_like(token_ref)
    rows, heads, size = out_ref.shape
    half = heads // 2
    core = lax.axis_index(AXIS) % 2
    flat = wide.reshape(rows * heads, size)
    share = half // own_ref.shape[0]
    skip = got_ref.shape[0] - half
    for j in range(half):
        g, r = j // share, j % share
        flat[pl.ds(core * half + j, rows, stride=heads), :] = own_ref[g, r * rows : (r + 1) * rows] * query_scale
        flat[pl.ds((1 - core) * half + j, rows, stride=heads), :] = got_ref[skip + j].astype(jnp.float32)
    out_ref[...] = wide[...].astype(out_ref.dtype)


def partial_kernel(own_ref, back_ref, side_ref, out_ref):
    out_ref[...] = own_ref[...] + back_ref[...].astype(jnp.float32) + side_ref[...].astype(jnp.float32)


def join_kernel(own_ref, side_ref, after, out_ref):
    odd = (lax.axis_index(AXIS) // 2) % 2 == 1
    side = side_ref[...].astype(jnp.float32)
    out_ref[...] = (own_ref[...] + jnp.where(odd, side, 0.0)).astype(out_ref.dtype)


def final_kv_kernel(part_ref, got_ref, back_r, side_r, after, out_k, out_v, wide):
    rows, heads, size = out_k.shape
    half = heads // 2
    device = lax.axis_index(AXIS)
    core = device % 2
    even = jnp.where((device // 2) % 2 == 0, 1.0, 0.0).astype(jnp.float32)
    flat = wide.reshape(rows * 2 * heads, size)
    for part in range(2):
        for j in range(half):
            n = part * half + j
            flat[pl.ds(part * heads + core * half + j, rows, stride=2 * heads), :] = part_ref[n]
            flat[pl.ds(part * heads + (1 - core) * half + j, rows, stride=2 * heads), :] = (
                got_ref[n].astype(jnp.float32)
                + back_r[n].astype(jnp.float32)
                + side_r[n].astype(jnp.float32) * even
            )
    out_k[...] = wide[:, :heads, :].astype(out_k.dtype)
    out_v[...] = wide[:, heads:, :].astype(out_v.dtype)


def shards(queries, key_rows, value_rows, attn_output, grad_output, log_norm):
    rows, heads, size = queries.shape
    groups = key_rows.shape[1]
    devices = lax.axis_size(AXIS)
    hops = W // rows
    assert hops == 4 and devices % 4 == 0
    low, f32 = jnp.bfloat16, jnp.float32
    device = lax.axis_index(AXIS)
    even = (device // 2) % 2 == 0

    def move(x, target):
        pairs = [(i, target(i)) for i in range(devices)]
        return lax.ppermute(x, AXIS, [(i, j) for i, j in pairs if j >= 0])

    ahead = lambda i: (i + hops) % devices
    behind = lambda i: (i - hops) % devices
    sibling = lambda i: i ^ 1
    beside = lambda i: i ^ 2

    shape = jax.ShapeDtypeStruct
    kv_block = (groups, rows, size)
    half_rows = heads * rows // 2
    row_block = (heads * rows // size, size)
    gq_block = (groups // 2, heads // groups * rows, size)

    hbm = pl.BlockSpec(memory_space=pltpu.HBM)
    vmem = pl.BlockSpec(memory_space=pltpu.VMEM)
    anywhere = pl.BlockSpec(memory_space=pl.ANY)
    hbm = pl.BlockSpec(memory_space=pltpu.HBM)
    vmem = pl.BlockSpec(memory_space=pltpu.VMEM)
    anywhere = pl.BlockSpec(memory_space=pl.ANY)

    def pin(x):
        return pltpu.with_memory_space_constraint(x, pltpu.HBM)

    kv_s, kv_give = call(
        pack_kv_kernel,
        "pack_kv",
        [shape(kv_block, low)] * 2,
        [pltpu.VMEM(key_rows.shape, low)] * 2
        + [pltpu.VMEM((rows, 2 * groups, size), f32), pltpu.SemaphoreType.DMA((2,))],
        in_specs=[hbm, hbm],
    )(pin(key_rows), pin(value_rows))
    kv_r = move(kv_give, sibling)
    two_s = move(kv_s, ahead)
    two_r = move(kv_r, ahead)
    q_s, g_s, rows_s, q_give, g_give = call(
        pack_q_kernel,
        "pack_q",
        [
            shape((half_rows, size), low),
            shape((half_rows, size), low),
            shape(row_block, f32),
            shape((half_rows + 3 * row_block[0], size), low),
            shape((half_rows, size), low),
        ],
        [pltpu.VMEM(queries.shape, low)] * 3
        + [pltpu.VMEM((rows, heads, size), f32), pltpu.VMEM(row_block, f32), pltpu.SemaphoreType.DMA((3,))],
        in_specs=[hbm, hbm, hbm, vmem, anywhere],
    )(pin(queries), pin(grad_output), pin(attn_output), log_norm, kv_r)
    q_r, g_r = move(q_give, sibling), move(g_give, sibling)
    two_s, rows_s = lax.optimization_barrier((two_s, rows_s))
    one_s = move(jnp.where(even, kv_s, two_s), beside)

    acc = [shape(gq_block, f32)] * 2
    grad_scratch = [pltpu.VMEM(kv_block, f32)]
    sides = (q_s, g_s, rows_s, q_r, g_r)
    grad_s, gq_s = call(
        own_side_kernel,
        "own_side",
        [shape(kv_block, f32), acc[0]],
        flops=0,
    )(kv_s, q_s, g_s, rows_s)
    far_s, gq_s, gq_r = call(
        functools.partial(far_kernel, True),
        "far_s",
        [shape(kv_block, low)] + acc,
        grad_scratch,
        flops=0,
    )(two_s, *sides, gq_s)
    back_s = move(far_s, behind)
    two_r, gq_s, gq_r = lax.optimization_barrier((two_r, gq_s, gq_r))
    one_r = move(jnp.where(even, kv_r, two_r), beside)
    far_r, gq_s, gq_r = call(
        functools.partial(far_kernel, False),
        "far_r",
        [shape(kv_block, f32)] + acc,
        grad_scratch,
        flops=0,
    )(two_r, *sides, gq_s, gq_r)
    near = functools.partial(
        call, near_kernel, out_shape=[shape(kv_block, low)] + acc, scratch=grad_scratch, flops=0
    )
    near_s, gq_s, gq_r = near(name="near_s")(one_s, *sides, gq_s, gq_r)
    side_s = move(near_s, lambda i: i - 2)
    near_r, gq_s, gq_r = near(name="near_r")(one_r, *sides, gq_s, gq_r)
    side_r = move(near_r, lambda i: i ^ 3 if i & 2 else i ^ 2)
    gq_s, back_s = lax.optimization_barrier((gq_s, back_s))
    own_s, own_r, gq_s, gq_r = call(
        own_rest_kernel, "own_rest", [shape(kv_block, f32)] * 2 + acc, flops=0
    )(kv_s, kv_r, *sides, grad_s, gq_s, gq_r)
    part = call(partial_kernel, "partial", shape(kv_block, f32), flops=LONG)(own_s, back_s, side_s)
    joined = call(join_kernel, "join", shape(kv_block, low), in_specs=[vmem, vmem, anywhere])(far_r, side_r, part)
    back_r = move(joined, lambda i: sibling(behind(i)))
    give = jnp.concatenate([own_r.astype(low), (gq_r * query_scale).astype(low).reshape(-1, rows, size)])
    got = move(give, sibling)
    grad_q, token = call(
        final_q_kernel,
        "final_q",
        [shape(queries.shape, low), shape((8, 128), f32)],
        [pltpu.VMEM((rows, heads, size), f32)],
    )(gq_s, got)
    grad_k, grad_v = call(
        final_kv_kernel,
        "final_kv",
        [shape(key_rows.shape, low), shape(value_rows.shape, low)],
        [pltpu.VMEM((rows, 2 * groups, size), f32)],
        in_specs=[vmem] * 4 + [anywhere],
    )(part, got, back_r, side_r, token)
    return grad_q, grad_k, grad_v


def solution(mesh):
    in_specs = (
        P("seq", None, None),
        P("seq", None, None),
        P("seq", None, None),
        P("seq", None, None),
        P("seq", None, None),
        P(None, "seq"),
    )
    out_specs = (P("seq", None, None), P("seq", None, None), P("seq", None, None))
    return jax.shard_map(shards, mesh=mesh, in_specs=in_specs, out_specs=out_specs, check_vma=False)
```

```python
import functools
import math

import jax
import jax.numpy as jnp
from jax import lax
from jax.experimental import pallas as pl
from jax.experimental.pallas import tpu as pltpu
from jax.sharding import PartitionSpec as P

W = 1024

query_scale = 168.0 ** (-0.5)
LOG2E = math.log2(math.e)
AXIS = "seq"
VMEM_LIMIT = 16 * 1024 * 1024
LONG = 10**10

NT = (((1,), (1,)), ((), ()))
NN = (((1,), (0,)), ((), ()))
TN = (((0,), (0,)), ((), ()))


def dot(a, b, dims):
    return lax.dot_general(a, b, dims, preferred_element_type=jnp.float32)


def call(kernel, name, out_shape, scratch=(), flops=0, in_specs=None):
    specs = {} if in_specs is None else {"in_specs": in_specs}
    return pl.pallas_call(
        kernel,
        out_shape=out_shape,
        scratch_shapes=list(scratch),
        name=name,
        cost_estimate=pl.CostEstimate(flops=flops, bytes_accessed=2 << 20, transcendentals=0),
        compiler_params=pltpu.CompilerParams(vmem_limit_bytes=VMEM_LIMIT),
        **specs,
    )


def fetch(pairs, sems):
    copies = [pltpu.make_async_copy(src, dst, sems.at[n]) for n, (src, dst) in enumerate(pairs)]
    for copy in copies:
        copy.start()
    return copies


def pack_kv_kernel(k_hbm, v_hbm, keep_ref, give_ref, k_ref, v_ref, wide, sems):
    copy_k, copy_v = fetch(((k_hbm, k_ref), (v_hbm, v_ref)), sems)
    rows, heads, _ = k_ref.shape
    half = heads // 2
    core = lax.axis_index(AXIS) % 2
    copy_k.wait()
    wide[:, :heads, :] = k_ref[...].astype(jnp.float32)
    copy_v.wait()
    wide[:, heads:, :] = v_ref[...].astype(jnp.float32)
    flat = wide.reshape(rows * 2 * heads, wide.shape[2])
    for out, side in ((keep_ref, core), (give_ref, 1 - core)):
        for part in range(2):
            for j in range(half):
                head = part * heads + side * half + j
                out[part * half + j] = flat[pl.ds(head, rows, stride=2 * heads), :].astype(out.dtype)


def split_three(x):
    parts = []
    for _ in range(3):
        part = x.astype(jnp.bfloat16)
        parts.append(part)
        x = x - part.astype(jnp.float32)
    return parts


def join_three(ref, start, count):
    high, mid, low = (ref[start + n * count : start + (n + 1) * count].astype(jnp.float32) for n in range(3))
    return high + mid + low


def pack_q_kernel(
    q_hbm,
    g_hbm,
    o_hbm,
    norm_ref,
    after,
    keep_q,
    keep_g,
    keep_rows,
    give_q,
    give_g,
    q_ref,
    g_ref,
    o_ref,
    wide,
    give_rows,
    sems,
):
    copy_q, copy_g, copy_o = fetch(((q_hbm, q_ref), (g_hbm, g_ref), (o_hbm, o_ref)), sems)
    rows, heads, size = q_ref.shape
    half = heads // 2
    pieces = rows // size
    core = lax.axis_index(AXIS) % 2
    ones = jnp.ones((8, size), jnp.float32)
    flat = wide.reshape(rows * heads, size)

    def spread(outs):
        for out, side in zip(outs, (core, 1 - core), strict=True):
            for j in range(half):
                block = flat[pl.ds(side * half + j, rows, stride=heads), :]
                out[j * rows : (j + 1) * rows] = block.astype(out.dtype)

    copy_q.wait()
    wide[...] = q_ref[...].astype(jnp.float32)
    spread((keep_q, give_q))
    copy_g.wait()
    wide[...] = g_ref[...].astype(jnp.float32)
    spread((keep_g, give_g))
    copy_o.wait()
    wide[...] = g_ref[...].astype(jnp.float32) * o_ref[...].astype(jnp.float32)
    for out, side in ((keep_rows, core), (give_rows, 1 - core)):
        for j in range(half):
            product = flat[pl.ds(side * half + j, rows, stride=heads), :]
            delta = lax.dot_general(
                ones, product, NT, precision=lax.Precision.HIGHEST, preferred_element_type=jnp.float32
            )
            norm = norm_ref[pl.ds(side * half + j, 1), :] * LOG2E
            for n in range(pieces):
                out[j * pieces + n : j * pieces + n + 1] = norm[:, n * size : (n + 1) * size]
                at = (half + j) * pieces + n
                out[at : at + 1] = delta[:1, n * size : (n + 1) * size]
    count = heads * pieces
    for n, part in enumerate(split_three(give_rows[...])):
        give_q[half * rows + n * count : half * rows + (n + 1) * count] = part


def tile(kv_ref, side, grad_ref, gq_in, gq_ref, offset, first):
    q_ref, g_ref, row_ref = side
    groups = kv_ref.shape[0] // 2
    rows, size = kv_ref.shape[1], kv_ref.shape[2]
    span = gq_ref.shape[1]
    share = span // rows
    pieces = span // size
    if row_ref is None:
        vectors = join_three(q_ref, g_ref.shape[0], 2 * groups * pieces)
    else:
        vectors = row_ref[...]

    def vector(at):
        return jnp.concatenate([vectors[at + n : at + n + 1] for n in range(pieces)], 1)

    for g in range(groups):
        k = kv_ref[g]
        v = kv_ref[groups + g]
        q = q_ref[g * span : (g + 1) * span]
        d = g_ref[g * span : (g + 1) * span]
        norm = vector(g * pieces)
        delta = vector((groups + g) * pieces)
        x = dot(k, q, NT) * (query_scale * LOG2E) - norm
        if offset is not None:
            key = lax.broadcasted_iota(jnp.int32, (rows, rows), 0)
            query = lax.broadcasted_iota(jnp.int32, (rows, rows), 1)
            gap = query - key + offset
            seen = (gap >= 0) & (gap < W)
            x = jnp.concatenate(
                [jnp.where(seen, x[:, j * rows : (j + 1) * rows], -jnp.inf) for j in range(share)], 1
            )
        p = jnp.exp2(x)
        ds = (p * (dot(v, d, NT) - delta)).astype(jnp.bfloat16)
        gv = dot(p.astype(jnp.bfloat16), d, NN)
        gk = dot(ds, q, NN)
        gq = dot(ds, k, TN)
        if first:
            grad_ref[g] = gk
            grad_ref[groups + g] = gv
        else:
            grad_ref[g] += gk
            grad_ref[groups + g] += gv
        gq_ref[g] = gq if gq_in is None else gq_in[g] + gq


def scale_keys(grad_ref):
    groups = grad_ref.shape[0] // 2
    grad_ref[:groups] = grad_ref[:groups] * query_scale


def own_side_kernel(kv_s, q_s, g_s, rows_s, grad_s, gq_s):
    tile(kv_s, (q_s, g_s, rows_s), grad_s, None, gq_s, 0, True)


def own_rest_kernel(kv_s, kv_r, q_s, g_s, rows_s, q_r, g_r, grad_s_in, gq_s_in, grad_s, grad_r, gq_s, gq_r):
    side_s, side_r = (q_s, g_s, rows_s), (q_r, g_r, None)
    core = lax.axis_index(AXIS) % 2
    grad_s[...] = grad_s_in[...]
    tile(kv_r, side_r, grad_r, None, gq_r, 0, True)

    @pl.when(core == 0)
    def _():
        tile(kv_s, side_r, grad_s, gq_r, gq_r, None, False)
        gq_s[...] = gq_s_in[...]

    @pl.when(core == 1)
    def _():
        tile(kv_r, side_s, grad_r, gq_s_in, gq_s, None, False)

    scale_keys(grad_s)
    scale_keys(grad_r)


def far_kernel(first, kv, q_s, g_s, rows_s, q_r, g_r, *refs):
    if first:
        gq_s_in, gq_r_in, out, gq_s, gq_r, grad = refs
        side_s, side_r, seen_by = (q_s, g_s, rows_s), (q_r, g_r, None), 1
    else:
        gq_r_in, gq_s_in, out, gq_r, gq_s, grad = refs
        side_s, side_r, seen_by = (q_r, g_r, None), (q_s, g_s, rows_s), 0
    device = lax.axis_index(AXIS)
    core = device % 2
    valid = device // 2 >= 2

    @pl.when(valid)
    def _():
        tile(kv, side_s, grad, gq_s_in, gq_s, W, True)

    @pl.when(valid & (core == seen_by))
    def _():
        tile(kv, side_r, grad, gq_r_in, gq_r, None, False)

    @pl.when(valid)
    def _():
        scale_keys(grad)
        out[...] = grad[...].astype(out.dtype)

    @pl.when(jnp.logical_not(valid))
    def _():
        out[...] = jnp.zeros_like(out)
        gq_s[...] = gq_s_in[...]

    @pl.when(jnp.logical_not(valid & (core == seen_by)))
    def _():
        gq_r[...] = gq_r_in[...]


def near_kernel(kv, q_s, g_s, rows_s, q_r, g_r, gq_s_in, gq_r_in, out, gq_s, gq_r, grad):
    side_s, side_r = (q_s, g_s, rows_s), (q_r, g_r, None)
    valid = lax.axis_index(AXIS) // 2 >= 1

    @pl.when(valid)
    def _():
        tile(kv, side_s, grad, gq_s_in, gq_s, None, True)
        tile(kv, side_r, grad, gq_r_in, gq_r, None, False)
        scale_keys(grad)
        out[...] = grad[...].astype(out.dtype)

    @pl.when(jnp.logical_not(valid))
    def _():
        out[...] = jnp.zeros_like(out)
        gq_s[...] = gq_s_in[...]
        gq_r[...] = gq_r_in[...]


def final_q_kernel(own_ref, got_ref, after, out_ref, token_ref, wide):
    token_ref[...] = jnp.zeros_like(token_ref)
    rows, heads, size = out_ref.shape
    half = heads // 2
    core = lax.axis_index(AXIS) % 2
    flat = wide.reshape(rows * heads, size)
    share = half // own_ref.shape[0]
    skip = got_ref.shape[0] - half
    for j in range(half):
        g, r = j // share, j % share
        flat[pl.ds(core * half + j, rows, stride=heads), :] = own_ref[g, r * rows : (r + 1) * rows] * query_scale
        flat[pl.ds((1 - core) * half + j, rows, stride=heads), :] = got_ref[skip + j].astype(jnp.float32)
    out_ref[...] = wide[...].astype(out_ref.dtype)


def partial_kernel(own_ref, back_ref, side_ref, out_ref):
    out_ref[...] = own_ref[...] + back_ref[...].astype(jnp.float32) + side_ref[...].astype(jnp.float32)


def final_kv_kernel(part_ref, got_ref, back_r, side_r, after, out_k, out_v, wide):
    rows, heads, size = out_k.shape
    half = heads // 2
    core = lax.axis_index(AXIS) % 2
    flat = wide.reshape(rows * 2 * heads, size)
    for part in range(2):
        for j in range(half):
            n = part * half + j
            flat[pl.ds(part * heads + core * half + j, rows, stride=2 * heads), :] = part_ref[n]
            flat[pl.ds(part * heads + (1 - core) * half + j, rows, stride=2 * heads), :] = (
                got_ref[n].astype(jnp.float32)
                + back_r[n].astype(jnp.float32)
                + side_r[n].astype(jnp.float32)
            )
    out_k[...] = wide[:, :heads, :].astype(out_k.dtype)
    out_v[...] = wide[:, heads:, :].astype(out_v.dtype)


def shards(queries, key_rows, value_rows, attn_output, grad_output, log_norm):
    rows, heads, size = queries.shape
    groups = key_rows.shape[1]
    devices = lax.axis_size(AXIS)
    hops = W // rows
    assert hops == 4 and devices % 4 == 0
    low, f32 = jnp.bfloat16, jnp.float32
    device = lax.axis_index(AXIS)
    even = (device // 2) % 2 == 0

    def move(x, target):
        pairs = [(i, target(i)) for i in range(devices)]
        return lax.ppermute(x, AXIS, [(i, j) for i, j in pairs if j >= 0])

    ahead = lambda i: (i + hops) % devices
    behind = lambda i: (i - hops) % devices
    sibling = lambda i: i ^ 1
    beside = lambda i: i ^ 2

    shape = jax.ShapeDtypeStruct
    kv_block = (groups, rows, size)
    half_rows = heads * rows // 2
    row_block = (heads * rows // size, size)
    gq_block = (groups // 2, heads // groups * rows, size)

    hbm = pl.BlockSpec(memory_space=pltpu.HBM)
    vmem = pl.BlockSpec(memory_space=pltpu.VMEM)
    anywhere = pl.BlockSpec(memory_space=pl.ANY)
    hbm = pl.BlockSpec(memory_space=pltpu.HBM)
    vmem = pl.BlockSpec(memory_space=pltpu.VMEM)
    anywhere = pl.BlockSpec(memory_space=pl.ANY)

    def pin(x):
        return pltpu.with_memory_space_constraint(x, pltpu.HBM)

    kv_s, kv_give = call(
        pack_kv_kernel,
        "pack_kv",
        [shape(kv_block, low)] * 2,
        [pltpu.VMEM(key_rows.shape, low)] * 2
        + [pltpu.VMEM((rows, 2 * groups, size), f32), pltpu.SemaphoreType.DMA((2,))],
        in_specs=[hbm, hbm],
    )(pin(key_rows), pin(value_rows))
    kv_r = move(kv_give, sibling)
    two_s = move(kv_s, ahead)
    two_r = move(kv_r, ahead)
    q_s, g_s, rows_s, q_give, g_give = call(
        pack_q_kernel,
        "pack_q",
        [
            shape((half_rows, size), low),
            shape((half_rows, size), low),
            shape(row_block, f32),
            shape((half_rows + 3 * row_block[0], size), low),
            shape((half_rows, size), low),
        ],
        [pltpu.VMEM(queries.shape, low)] * 3
        + [pltpu.VMEM((rows, heads, size), f32), pltpu.VMEM(row_block, f32), pltpu.SemaphoreType.DMA((3,))],
        in_specs=[hbm, hbm, hbm, vmem, anywhere],
    )(pin(queries), pin(grad_output), pin(attn_output), log_norm, kv_r)
    q_r, g_r = move(q_give, sibling), move(g_give, sibling)
    acc = [shape(gq_block, f32)] * 2
    grad_scratch = [pltpu.VMEM(kv_block, f32)]
    two_s, rows_s = lax.optimization_barrier((two_s, rows_s))
    one_s = move(jnp.where(even, kv_s, two_s), beside)
    sides = (q_s, g_s, rows_s, q_r, g_r)
    grad_s, gq_s = call(own_side_kernel, "own_side", [shape(kv_block, f32), acc[0]], flops=0)(
        kv_s, q_s, g_s, rows_s
    )
    own_s, own_r, gq_s, gq_r = call(own_rest_kernel, "own_rest", [shape(kv_block, f32)] * 2 + acc, flops=0)(
        kv_s, kv_r, *sides, grad_s, gq_s
    )
    far_s, gq_s, gq_r = call(
        functools.partial(far_kernel, True), "far_s", [shape(kv_block, low)] + acc, grad_scratch
    )(two_s, *sides, gq_s, gq_r)
    back_s = move(far_s, behind)
    two_r, gq_s, gq_r = lax.optimization_barrier((two_r, gq_s, gq_r))
    one_r = move(jnp.where(even, kv_r, two_r), beside)
    far_r, gq_s, gq_r = call(
        functools.partial(far_kernel, False),
        "far_r",
        [shape(kv_block, low)] + acc,
        grad_scratch,
    )(two_r, *sides, gq_s, gq_r)
    back_r = move(far_r, lambda i: sibling(behind(i)))
    near = functools.partial(call, near_kernel, out_shape=[shape(kv_block, low)] + acc, scratch=grad_scratch)
    near_s, gq_s, gq_r = near(name="near_s")(one_s, *sides, gq_s, gq_r)
    side_s = move(near_s, lambda i: i - 2)
    one_r, back_s = lax.optimization_barrier((one_r, back_s))
    near_r, gq_s, gq_r = near(name="near_r")(one_r, *sides, gq_s, gq_r)
    side_r = move(near_r, lambda i: sibling(i - 2) if i >= 2 else -1)

    part = call(partial_kernel, "partial", shape(kv_block, f32), flops=LONG)(own_s, back_s, side_s)
    give = jnp.concatenate([own_r.astype(low), (gq_r * query_scale).astype(low).reshape(-1, rows, size)])
    got = move(give, sibling)
    grad_q, token = call(
        final_q_kernel,
        "final_q",
        [shape(queries.shape, low), shape((8, 128), f32)],
        [pltpu.VMEM((rows, heads, size), f32)],
        in_specs=[vmem, vmem, anywhere],
    )(gq_s, got, part)
    grad_k, grad_v = call(
        final_kv_kernel,
        "final_kv",
        [shape(key_rows.shape, low), shape(value_rows.shape, low)],
        [pltpu.VMEM((rows, 2 * groups, size), f32)],
        in_specs=[vmem] * 4 + [anywhere],
    )(part, got, back_r, side_r, token)
    return grad_q, grad_k, grad_v


def solution(mesh):
    in_specs = (
        P("seq", None, None),
        P("seq", None, None),
        P("seq", None, None),
        P("seq", None, None),
        P("seq", None, None),
        P(None, "seq"),
    )
    out_specs = (P("seq", None, None), P("seq", None, None), P("seq", None, None))
    return jax.shard_map(shards, mesh=mesh, in_specs=in_specs, out_specs=out_specs, check_vma=False)
```

```python
import functools
import math

import jax
import jax.numpy as jnp
from jax import lax
from jax.experimental import pallas as pl
from jax.experimental.pallas import tpu as pltpu
from jax.sharding import PartitionSpec as P

W = 1024

query_scale = 168.0 ** (-0.5)
LOG2E = math.log2(math.e)
AXIS = "seq"
VMEM_LIMIT = 16 * 1024 * 1024
LONG = 10**10

NT = (((1,), (1,)), ((), ()))
NN = (((1,), (0,)), ((), ()))
TN = (((0,), (0,)), ((), ()))


def dot(a, b, dims):
    return lax.dot_general(a, b, dims, preferred_element_type=jnp.float32)


def call(kernel, name, out_shape, scratch=(), flops=0, in_specs=None):
    specs = {} if in_specs is None else {"in_specs": in_specs}
    return pl.pallas_call(
        kernel,
        out_shape=out_shape,
        scratch_shapes=list(scratch),
        name=name,
        cost_estimate=pl.CostEstimate(flops=flops, bytes_accessed=2 << 20, transcendentals=0),
        compiler_params=pltpu.CompilerParams(vmem_limit_bytes=VMEM_LIMIT),
        **specs,
    )


def fetch(pairs, sems):
    copies = [pltpu.make_async_copy(src, dst, sems.at[n]) for n, (src, dst) in enumerate(pairs)]
    for copy in copies:
        copy.start()
    return copies


def pack_kv_kernel(k_hbm, v_hbm, keep_ref, give_ref, k_ref, v_ref, wide, sems):
    copy_k, copy_v = fetch(((k_hbm, k_ref), (v_hbm, v_ref)), sems)
    rows, heads, _ = k_ref.shape
    half = heads // 2
    core = lax.axis_index(AXIS) % 2
    copy_k.wait()
    wide[:, :heads, :] = k_ref[...].astype(jnp.float32)
    copy_v.wait()
    wide[:, heads:, :] = v_ref[...].astype(jnp.float32)
    flat = wide.reshape(rows * 2 * heads, wide.shape[2])
    for out, side in ((keep_ref, core), (give_ref, 1 - core)):
        for part in range(2):
            for j in range(half):
                head = part * heads + side * half + j
                out[part * half + j] = flat[pl.ds(head, rows, stride=2 * heads), :].astype(out.dtype)


def split_three(x):
    parts = []
    for _ in range(3):
        part = x.astype(jnp.bfloat16)
        parts.append(part)
        x = x - part.astype(jnp.float32)
    return parts


def join_three(ref, start, count):
    high, mid, low = (ref[start + n * count : start + (n + 1) * count].astype(jnp.float32) for n in range(3))
    return high + mid + low


def pack_q_kernel(
    q_hbm,
    g_hbm,
    o_hbm,
    norm_ref,
    after,
    keep_q,
    keep_g,
    keep_rows,
    give_q,
    give_g,
    q_ref,
    g_ref,
    o_ref,
    wide,
    give_rows,
    sems,
):
    copy_q, copy_g, copy_o = fetch(((q_hbm, q_ref), (g_hbm, g_ref), (o_hbm, o_ref)), sems)
    rows, heads, size = q_ref.shape
    half = heads // 2
    pieces = rows // size
    core = lax.axis_index(AXIS) % 2
    ones = jnp.ones((8, size), jnp.float32)
    flat = wide.reshape(rows * heads, size)

    def spread(outs):
        for out, side in zip(outs, (core, 1 - core), strict=True):
            for j in range(half):
                block = flat[pl.ds(side * half + j, rows, stride=heads), :]
                out[j * rows : (j + 1) * rows] = block.astype(out.dtype)

    copy_q.wait()
    wide[...] = q_ref[...].astype(jnp.float32)
    spread((keep_q, give_q))
    copy_g.wait()
    wide[...] = g_ref[...].astype(jnp.float32)
    spread((keep_g, give_g))
    copy_o.wait()
    wide[...] = g_ref[...].astype(jnp.float32) * o_ref[...].astype(jnp.float32)
    for out, side in ((keep_rows, core), (give_rows, 1 - core)):
        for j in range(half):
            product = flat[pl.ds(side * half + j, rows, stride=heads), :]
            delta = lax.dot_general(
                ones, product, NT, precision=lax.Precision.HIGHEST, preferred_element_type=jnp.float32
            )
            norm = norm_ref[pl.ds(side * half + j, 1), :] * LOG2E
            for n in range(pieces):
                out[j * pieces + n : j * pieces + n + 1] = norm[:, n * size : (n + 1) * size]
                at = (half + j) * pieces + n
                out[at : at + 1] = delta[:1, n * size : (n + 1) * size]
    count = heads * pieces
    for n, part in enumerate(split_three(give_rows[...])):
        give_q[half * rows + n * count : half * rows + (n + 1) * count] = part


def tile(kv_ref, side, grad_ref, gq_in, gq_ref, offset, first):
    q_ref, g_ref, row_ref = side
    groups = kv_ref.shape[0] // 2
    rows, size = kv_ref.shape[1], kv_ref.shape[2]
    span = gq_ref.shape[1]
    share = span // rows
    pieces = span // size
    if row_ref is None:
        vectors = join_three(q_ref, g_ref.shape[0], 2 * groups * pieces)
    else:
        vectors = row_ref[...]

    def vector(at):
        return jnp.concatenate([vectors[at + n : at + n + 1] for n in range(pieces)], 1)

    for g in range(groups):
        k = kv_ref[g]
        v = kv_ref[groups + g]
        q = q_ref[g * span : (g + 1) * span]
        d = g_ref[g * span : (g + 1) * span]
        norm = vector(g * pieces)
        delta = vector((groups + g) * pieces)
        x = dot(k, q, NT) * (query_scale * LOG2E) - norm
        if offset is not None:
            key = lax.broadcasted_iota(jnp.int32, (rows, rows), 0)
            query = lax.broadcasted_iota(jnp.int32, (rows, rows), 1)
            gap = query - key + offset
            seen = (gap >= 0) & (gap < W)
            x = jnp.concatenate(
                [jnp.where(seen, x[:, j * rows : (j + 1) * rows], -jnp.inf) for j in range(share)], 1
            )
        p = jnp.exp2(x)
        ds = (p * (dot(v, d, NT) - delta)).astype(jnp.bfloat16)
        gv = dot(p.astype(jnp.bfloat16), d, NN)
        gk = dot(ds, q, NN)
        gq = dot(ds, k, TN)
        if first:
            grad_ref[g] = gk
            grad_ref[groups + g] = gv
        else:
            grad_ref[g] += gk
            grad_ref[groups + g] += gv
        gq_ref[g] = gq if gq_in is None else gq_in[g] + gq


def scale_keys(grad_ref):
    groups = grad_ref.shape[0] // 2
    grad_ref[:groups] = grad_ref[:groups] * query_scale


def own_side_kernel(kv_s, q_s, g_s, rows_s, grad_s, gq_s):
    tile(kv_s, (q_s, g_s, rows_s), grad_s, None, gq_s, 0, True)


def own_rest_kernel(kv_s, kv_r, q_s, g_s, rows_s, q_r, g_r, grad_s_in, gq_s_in, grad_s, grad_r, gq_s, gq_r):
    side_s, side_r = (q_s, g_s, rows_s), (q_r, g_r, None)
    core = lax.axis_index(AXIS) % 2
    grad_s[...] = grad_s_in[...]
    tile(kv_r, side_r, grad_r, None, gq_r, 0, True)

    @pl.when(core == 0)
    def _():
        tile(kv_s, side_r, grad_s, gq_r, gq_r, None, False)
        gq_s[...] = gq_s_in[...]

    @pl.when(core == 1)
    def _():
        tile(kv_r, side_s, grad_r, gq_s_in, gq_s, None, False)

    scale_keys(grad_s)
    scale_keys(grad_r)


def far_kernel(first, kv, q_s, g_s, rows_s, q_r, g_r, *refs):
    if first:
        gq_s_in, gq_r_in, out, gq_s, gq_r, grad = refs
        side_s, side_r, seen_by = (q_s, g_s, rows_s), (q_r, g_r, None), 1
    else:
        gq_r_in, gq_s_in, out, gq_r, gq_s, grad = refs
        side_s, side_r, seen_by = (q_r, g_r, None), (q_s, g_s, rows_s), 0
    device = lax.axis_index(AXIS)
    core = device % 2
    valid = device // 2 >= 2

    @pl.when(valid)
    def _():
        tile(kv, side_s, grad, gq_s_in, gq_s, W, True)

    @pl.when(valid & (core == seen_by))
    def _():
        tile(kv, side_r, grad, gq_r_in, gq_r, None, False)

    @pl.when(valid)
    def _():
        scale_keys(grad)
        out[...] = grad[...].astype(out.dtype)

    @pl.when(jnp.logical_not(valid))
    def _():
        out[...] = jnp.zeros_like(out)
        gq_s[...] = gq_s_in[...]

    @pl.when(jnp.logical_not(valid & (core == seen_by)))
    def _():
        gq_r[...] = gq_r_in[...]


def near_kernel(kv, q_s, g_s, rows_s, q_r, g_r, gq_s_in, gq_r_in, out, gq_s, gq_r, grad):
    side_s, side_r = (q_s, g_s, rows_s), (q_r, g_r, None)
    valid = lax.axis_index(AXIS) // 2 >= 1

    @pl.when(valid)
    def _():
        tile(kv, side_s, grad, gq_s_in, gq_s, None, True)
        tile(kv, side_r, grad, gq_r_in, gq_r, None, False)
        scale_keys(grad)
        out[...] = grad[...].astype(out.dtype)

    @pl.when(jnp.logical_not(valid))
    def _():
        out[...] = jnp.zeros_like(out)
        gq_s[...] = gq_s_in[...]
        gq_r[...] = gq_r_in[...]


def final_q_kernel(own_ref, got_ref, after, out_ref, token_ref, wide):
    token_ref[...] = jnp.zeros_like(token_ref)
    rows, heads, size = out_ref.shape
    half = heads // 2
    core = lax.axis_index(AXIS) % 2
    flat = wide.reshape(rows * heads, size)
    share = half // own_ref.shape[0]
    skip = got_ref.shape[0] - half
    for j in range(half):
        g, r = j // share, j % share
        flat[pl.ds(core * half + j, rows, stride=heads), :] = own_ref[g, r * rows : (r + 1) * rows] * query_scale
        flat[pl.ds((1 - core) * half + j, rows, stride=heads), :] = got_ref[skip + j].astype(jnp.float32)
    out_ref[...] = wide[...].astype(out_ref.dtype)


def partial_kernel(own_ref, back_ref, out_ref):
    out_ref[...] = own_ref[...] + back_ref[...].astype(jnp.float32)


def final_kv_kernel(part_ref, got_ref, back_r, side_s, side_r, after, out_k, out_v, wide):
    rows, heads, size = out_k.shape
    half = heads // 2
    core = lax.axis_index(AXIS) % 2
    flat = wide.reshape(rows * 2 * heads, size)
    for part in range(2):
        for j in range(half):
            n = part * half + j
            flat[pl.ds(part * heads + core * half + j, rows, stride=2 * heads), :] = part_ref[n] + side_s[n].astype(
                jnp.float32
            )
            flat[pl.ds(part * heads + (1 - core) * half + j, rows, stride=2 * heads), :] = (
                got_ref[n].astype(jnp.float32)
                + back_r[n].astype(jnp.float32)
                + side_r[n].astype(jnp.float32)
            )
    out_k[...] = wide[:, :heads, :].astype(out_k.dtype)
    out_v[...] = wide[:, heads:, :].astype(out_v.dtype)


def shards(queries, key_rows, value_rows, attn_output, grad_output, log_norm):
    rows, heads, size = queries.shape
    groups = key_rows.shape[1]
    devices = lax.axis_size(AXIS)
    hops = W // rows
    assert hops == 4 and devices % 4 == 0
    low, f32 = jnp.bfloat16, jnp.float32
    device = lax.axis_index(AXIS)
    even = (device // 2) % 2 == 0

    def move(x, target):
        pairs = [(i, target(i)) for i in range(devices)]
        return lax.ppermute(x, AXIS, [(i, j) for i, j in pairs if j >= 0])

    ahead = lambda i: (i + hops) % devices
    behind = lambda i: (i - hops) % devices
    sibling = lambda i: i ^ 1
    beside = lambda i: i ^ 2

    shape = jax.ShapeDtypeStruct
    kv_block = (groups, rows, size)
    half_rows = heads * rows // 2
    row_block = (heads * rows // size, size)
    gq_block = (groups // 2, heads // groups * rows, size)

    hbm = pl.BlockSpec(memory_space=pltpu.HBM)
    vmem = pl.BlockSpec(memory_space=pltpu.VMEM)
    anywhere = pl.BlockSpec(memory_space=pl.ANY)
    hbm = pl.BlockSpec(memory_space=pltpu.HBM)
    vmem = pl.BlockSpec(memory_space=pltpu.VMEM)
    anywhere = pl.BlockSpec(memory_space=pl.ANY)

    def pin(x):
        return pltpu.with_memory_space_constraint(x, pltpu.HBM)

    kv_s, kv_give = call(
        pack_kv_kernel,
        "pack_kv",
        [shape(kv_block, low)] * 2,
        [pltpu.VMEM(key_rows.shape, low)] * 2
        + [pltpu.VMEM((rows, 2 * groups, size), f32), pltpu.SemaphoreType.DMA((2,))],
        in_specs=[hbm, hbm],
    )(pin(key_rows), pin(value_rows))
    kv_r = move(kv_give, sibling)
    two_s = move(kv_s, ahead)
    two_r = move(kv_r, ahead)
    q_s, g_s, rows_s, q_give, g_give = call(
        pack_q_kernel,
        "pack_q",
        [
            shape((half_rows, size), low),
            shape((half_rows, size), low),
            shape(row_block, f32),
            shape((half_rows + 3 * row_block[0], size), low),
            shape((half_rows, size), low),
        ],
        [pltpu.VMEM(queries.shape, low)] * 3
        + [pltpu.VMEM((rows, heads, size), f32), pltpu.VMEM(row_block, f32), pltpu.SemaphoreType.DMA((3,))],
        in_specs=[hbm, hbm, hbm, vmem, anywhere],
    )(pin(queries), pin(grad_output), pin(attn_output), log_norm, kv_r)
    q_r, g_r = move(q_give, sibling), move(g_give, sibling)
    acc = [shape(gq_block, f32)] * 2
    grad_scratch = [pltpu.VMEM(kv_block, f32)]
    two_s, rows_s = lax.optimization_barrier((two_s, rows_s))
    one_s = move(jnp.where(even, kv_s, two_s), beside)
    sides = (q_s, g_s, rows_s, q_r, g_r)
    grad_s, gq_s = call(own_side_kernel, "own_side", [shape(kv_block, f32), acc[0]], flops=0)(
        kv_s, q_s, g_s, rows_s
    )
    own_s, own_r, gq_s, gq_r = call(own_rest_kernel, "own_rest", [shape(kv_block, f32)] * 2 + acc, flops=0)(
        kv_s, kv_r, *sides, grad_s, gq_s
    )
    far_s, gq_s, gq_r = call(
        functools.partial(far_kernel, True), "far_s", [shape(kv_block, low)] + acc, grad_scratch
    )(two_s, *sides, gq_s, gq_r)
    back_s = move(far_s, behind)
    two_r, gq_s, gq_r = lax.optimization_barrier((two_r, gq_s, gq_r))
    one_r = move(jnp.where(even, kv_r, two_r), beside)
    far_r, gq_s, gq_r = call(
        functools.partial(far_kernel, False),
        "far_r",
        [shape(kv_block, low)] + acc,
        grad_scratch,
    )(two_r, *sides, gq_s, gq_r)
    back_r = move(far_r, lambda i: sibling(behind(i)))
    near = functools.partial(call, near_kernel, out_shape=[shape(kv_block, low)] + acc, scratch=grad_scratch)
    near_s, gq_s, gq_r = near(name="near_s")(one_s, *sides, gq_s, gq_r)
    side_s = move(near_s, lambda i: i - 2)
    near_r, gq_s, gq_r = near(name="near_r")(one_r, *sides, gq_s, gq_r)
    side_r = move(near_r, lambda i: sibling(i - 2) if i >= 2 else -1)

    part = call(partial_kernel, "partial", shape(kv_block, f32), flops=LONG)(own_s, back_s)
    give = jnp.concatenate([own_r.astype(low), (gq_r * query_scale).astype(low).reshape(-1, rows, size)])
    got = move(give, sibling)
    grad_q, token = call(
        final_q_kernel,
        "final_q",
        [shape(queries.shape, low), shape((8, 128), f32)],
        [pltpu.VMEM((rows, heads, size), f32)],
        in_specs=[vmem, vmem, anywhere],
    )(gq_s, got, part)
    grad_k, grad_v = call(
        final_kv_kernel,
        "final_kv",
        [shape(key_rows.shape, low), shape(value_rows.shape, low)],
        [pltpu.VMEM((rows, 2 * groups, size), f32)],
        in_specs=[vmem] * 5 + [anywhere],
    )(part, got, back_r, side_s, side_r, token)
    return grad_q, grad_k, grad_v


def solution(mesh):
    in_specs = (
        P("seq", None, None),
        P("seq", None, None),
        P("seq", None, None),
        P("seq", None, None),
        P("seq", None, None),
        P(None, "seq"),
    )
    out_specs = (P("seq", None, None), P("seq", None, None), P("seq", None, None))
    return jax.shard_map(shards, mesh=mesh, in_specs=in_specs, out_specs=out_specs, check_vma=False)
```

```python
import functools
import math

import jax
import jax.numpy as jnp
from jax import lax
from jax.experimental import pallas as pl
from jax.experimental.pallas import tpu as pltpu
from jax.sharding import PartitionSpec as P

W = 1024

query_scale = 168.0 ** (-0.5)
LOG2E = math.log2(math.e)
AXIS = "seq"
VMEM_LIMIT = 16 * 1024 * 1024
LONG = 10**10

NT = (((1,), (1,)), ((), ()))
NN = (((1,), (0,)), ((), ()))
TN = (((0,), (0,)), ((), ()))


def dot(a, b, dims):
    return lax.dot_general(a, b, dims, preferred_element_type=jnp.float32)


def call(kernel, name, out_shape, scratch=(), flops=0, in_specs=None):
    specs = {} if in_specs is None else {"in_specs": in_specs}
    return pl.pallas_call(
        kernel,
        out_shape=out_shape,
        scratch_shapes=list(scratch),
        name=name,
        cost_estimate=pl.CostEstimate(flops=flops, bytes_accessed=2 << 20, transcendentals=0),
        compiler_params=pltpu.CompilerParams(vmem_limit_bytes=VMEM_LIMIT),
        **specs,
    )


def fetch(pairs, sems):
    copies = [pltpu.make_async_copy(src, dst, sems.at[n]) for n, (src, dst) in enumerate(pairs)]
    for copy in copies:
        copy.start()
    return copies


def pack_kv_kernel(k_hbm, v_hbm, keep_ref, give_ref, k_ref, v_ref, wide, sems):
    copy_k, copy_v = fetch(((k_hbm, k_ref), (v_hbm, v_ref)), sems)
    rows, heads, _ = k_ref.shape
    half = heads // 2
    core = lax.axis_index(AXIS) % 2
    copy_k.wait()
    wide[:, :heads, :] = k_ref[...].astype(jnp.float32)
    copy_v.wait()
    wide[:, heads:, :] = v_ref[...].astype(jnp.float32)
    flat = wide.reshape(rows * 2 * heads, wide.shape[2])
    for out, side in ((keep_ref, core), (give_ref, 1 - core)):
        for part in range(2):
            for j in range(half):
                head = part * heads + side * half + j
                out[part * half + j] = flat[pl.ds(head, rows, stride=2 * heads), :].astype(out.dtype)


def split_three(x):
    parts = []
    for _ in range(3):
        part = x.astype(jnp.bfloat16)
        parts.append(part)
        x = x - part.astype(jnp.float32)
    return parts


def join_three(ref, start, count):
    high, mid, low = (ref[start + n * count : start + (n + 1) * count].astype(jnp.float32) for n in range(3))
    return high + mid + low


def pack_q_kernel(
    q_hbm,
    g_hbm,
    o_hbm,
    norm_ref,
    after,
    keep_q,
    keep_g,
    keep_rows,
    give_q,
    give_g,
    q_ref,
    g_ref,
    o_ref,
    wide,
    give_rows,
    sems,
):
    copy_q, copy_g, copy_o = fetch(((q_hbm, q_ref), (g_hbm, g_ref), (o_hbm, o_ref)), sems)
    rows, heads, size = q_ref.shape
    half = heads // 2
    pieces = rows // size
    core = lax.axis_index(AXIS) % 2
    ones = jnp.ones((8, size), jnp.float32)
    flat = wide.reshape(rows * heads, size)

    def spread(outs):
        for out, side in zip(outs, (core, 1 - core), strict=True):
            for j in range(half):
                block = flat[pl.ds(side * half + j, rows, stride=heads), :]
                out[j * rows : (j + 1) * rows] = block.astype(out.dtype)

    copy_q.wait()
    wide[...] = q_ref[...].astype(jnp.float32)
    spread((keep_q, give_q))
    copy_g.wait()
    wide[...] = g_ref[...].astype(jnp.float32)
    spread((keep_g, give_g))
    copy_o.wait()
    wide[...] = g_ref[...].astype(jnp.float32) * o_ref[...].astype(jnp.float32)
    for out, side in ((keep_rows, core), (give_rows, 1 - core)):
        for j in range(half):
            product = flat[pl.ds(side * half + j, rows, stride=heads), :]
            delta = lax.dot_general(
                ones, product, NT, precision=lax.Precision.HIGHEST, preferred_element_type=jnp.float32
            )
            norm = norm_ref[pl.ds(side * half + j, 1), :] * LOG2E
            for n in range(pieces):
                out[j * pieces + n : j * pieces + n + 1] = norm[:, n * size : (n + 1) * size]
                at = (half + j) * pieces + n
                out[at : at + 1] = delta[:1, n * size : (n + 1) * size]
    count = heads * pieces
    for n, part in enumerate(split_three(give_rows[...])):
        give_q[half * rows + n * count : half * rows + (n + 1) * count] = part


def tile(kv_ref, side, grad_ref, gq_in, gq_ref, offset, first):
    q_ref, g_ref, row_ref = side
    groups = kv_ref.shape[0] // 2
    rows, size = kv_ref.shape[1], kv_ref.shape[2]
    span = gq_ref.shape[1]
    share = span // rows
    pieces = span // size
    if row_ref is None:
        vectors = join_three(q_ref, g_ref.shape[0], 2 * groups * pieces)
    else:
        vectors = row_ref[...]

    def vector(at):
        return jnp.concatenate([vectors[at + n : at + n + 1] for n in range(pieces)], 1)

    for g in range(groups):
        k = kv_ref[g]
        v = kv_ref[groups + g]
        q = q_ref[g * span : (g + 1) * span]
        d = g_ref[g * span : (g + 1) * span]
        norm = vector(g * pieces)
        delta = vector((groups + g) * pieces)
        x = dot(k, q, NT) * (query_scale * LOG2E) - norm
        if offset is not None:
            key = lax.broadcasted_iota(jnp.int32, (rows, rows), 0)
            query = lax.broadcasted_iota(jnp.int32, (rows, rows), 1)
            gap = query - key + offset
            seen = (gap >= 0) & (gap < W)
            x = jnp.concatenate(
                [jnp.where(seen, x[:, j * rows : (j + 1) * rows], -jnp.inf) for j in range(share)], 1
            )
        p = jnp.exp2(x)
        ds = (p * (dot(v, d, NT) - delta)).astype(jnp.bfloat16)
        gv = dot(p.astype(jnp.bfloat16), d, NN)
        gk = dot(ds, q, NN)
        gq = dot(ds, k, TN)
        if first:
            grad_ref[g] = gk
            grad_ref[groups + g] = gv
        else:
            grad_ref[g] += gk
            grad_ref[groups + g] += gv
        gq_ref[g] = gq if gq_in is None else gq_in[g] + gq


def scale_keys(grad_ref):
    groups = grad_ref.shape[0] // 2
    grad_ref[:groups] = grad_ref[:groups] * query_scale


def own_side_kernel(kv_s, q_s, g_s, rows_s, grad_s, gq_s):
    tile(kv_s, (q_s, g_s, rows_s), grad_s, None, gq_s, 0, True)


def own_rest_kernel(kv_s, kv_r, q_s, g_s, rows_s, q_r, g_r, grad_s_in, gq_s_in, grad_s, grad_r, gq_s, gq_r):
    side_s, side_r = (q_s, g_s, rows_s), (q_r, g_r, None)
    core = lax.axis_index(AXIS) % 2
    grad_s[...] = grad_s_in[...]
    tile(kv_r, side_r, grad_r, None, gq_r, 0, True)

    @pl.when(core == 0)
    def _():
        tile(kv_s, side_r, grad_s, gq_r, gq_r, None, False)
        gq_s[...] = gq_s_in[...]

    @pl.when(core == 1)
    def _():
        tile(kv_r, side_s, grad_r, gq_s_in, gq_s, None, False)

    scale_keys(grad_s)
    scale_keys(grad_r)


def far_kernel(first, kv, q_s, g_s, rows_s, q_r, g_r, *refs):
    if first:
        gq_s_in, gq_r_in, out, gq_s, gq_r, grad = refs
        side_s, side_r, seen_by = (q_s, g_s, rows_s), (q_r, g_r, None), 1
    else:
        gq_r_in, gq_s_in, out, gq_r, gq_s, grad = refs
        side_s, side_r, seen_by = (q_r, g_r, None), (q_s, g_s, rows_s), 0
    device = lax.axis_index(AXIS)
    core = device % 2
    valid = device // 2 >= 2

    @pl.when(valid)
    def _():
        tile(kv, side_s, grad, gq_s_in, gq_s, W, True)

    @pl.when(valid & (core == seen_by))
    def _():
        tile(kv, side_r, grad, gq_r_in, gq_r, None, False)

    @pl.when(valid)
    def _():
        scale_keys(grad)
        out[...] = grad[...].astype(out.dtype)

    @pl.when(jnp.logical_not(valid))
    def _():
        out[...] = jnp.zeros_like(out)
        gq_s[...] = gq_s_in[...]

    @pl.when(jnp.logical_not(valid & (core == seen_by)))
    def _():
        gq_r[...] = gq_r_in[...]


def near_kernel(kv, q_s, g_s, rows_s, q_r, g_r, gq_s_in, gq_r_in, out, gq_s, gq_r, grad):
    side_s, side_r = (q_s, g_s, rows_s), (q_r, g_r, None)
    valid = lax.axis_index(AXIS) // 2 >= 1

    @pl.when(valid)
    def _():
        tile(kv, side_s, grad, gq_s_in, gq_s, None, True)
        tile(kv, side_r, grad, gq_r_in, gq_r, None, False)
        scale_keys(grad)
        out[...] = grad[...].astype(out.dtype)

    @pl.when(jnp.logical_not(valid))
    def _():
        out[...] = jnp.zeros_like(out)
        gq_s[...] = gq_s_in[...]
        gq_r[...] = gq_r_in[...]


def final_q_kernel(own_ref, got_ref, after, out_ref, token_ref, wide):
    token_ref[...] = jnp.zeros_like(token_ref)
    rows, heads, size = out_ref.shape
    half = heads // 2
    core = lax.axis_index(AXIS) % 2
    flat = wide.reshape(rows * heads, size)
    share = half // own_ref.shape[0]
    skip = got_ref.shape[0] - half
    for j in range(half):
        g, r = j // share, j % share
        flat[pl.ds(core * half + j, rows, stride=heads), :] = own_ref[g, r * rows : (r + 1) * rows] * query_scale
        flat[pl.ds((1 - core) * half + j, rows, stride=heads), :] = got_ref[skip + j].astype(jnp.float32)
    out_ref[...] = wide[...].astype(out_ref.dtype)


def partial_kernel(own_ref, back_ref, out_ref):
    out_ref[...] = own_ref[...] + back_ref[...].astype(jnp.float32)


def final_kv_kernel(part_ref, got_ref, back_r, side_s, side_r, after, out_k, out_v, wide):
    rows, heads, size = out_k.shape
    half = heads // 2
    core = lax.axis_index(AXIS) % 2
    flat = wide.reshape(rows * 2 * heads, size)
    for part in range(2):
        for j in range(half):
            n = part * half + j
            flat[pl.ds(part * heads + core * half + j, rows, stride=2 * heads), :] = part_ref[n] + side_s[n].astype(
                jnp.float32
            )
            flat[pl.ds(part * heads + (1 - core) * half + j, rows, stride=2 * heads), :] = (
                got_ref[n].astype(jnp.float32)
                + back_r[n].astype(jnp.float32)
                + side_r[n].astype(jnp.float32)
            )
    out_k[...] = wide[:, :heads, :].astype(out_k.dtype)
    out_v[...] = wide[:, heads:, :].astype(out_v.dtype)


def shards(queries, key_rows, value_rows, attn_output, grad_output, log_norm):
    rows, heads, size = queries.shape
    groups = key_rows.shape[1]
    devices = lax.axis_size(AXIS)
    hops = W // rows
    assert hops == 4 and devices % 4 == 0
    low, f32 = jnp.bfloat16, jnp.float32
    device = lax.axis_index(AXIS)
    even = (device // 2) % 2 == 0

    def move(x, target):
        pairs = [(i, target(i)) for i in range(devices)]
        return lax.ppermute(x, AXIS, [(i, j) for i, j in pairs if j >= 0])

    ahead = lambda i: (i + hops) % devices
    behind = lambda i: (i - hops) % devices
    sibling = lambda i: i ^ 1
    beside = lambda i: i ^ 2

    shape = jax.ShapeDtypeStruct
    kv_block = (groups, rows, size)
    half_rows = heads * rows // 2
    row_block = (heads * rows // size, size)
    gq_block = (groups // 2, heads // groups * rows, size)

    hbm = pl.BlockSpec(memory_space=pltpu.HBM)
    vmem = pl.BlockSpec(memory_space=pltpu.VMEM)
    anywhere = pl.BlockSpec(memory_space=pl.ANY)
    hbm = pl.BlockSpec(memory_space=pltpu.HBM)
    vmem = pl.BlockSpec(memory_space=pltpu.VMEM)
    anywhere = pl.BlockSpec(memory_space=pl.ANY)

    def pin(x):
        return pltpu.with_memory_space_constraint(x, pltpu.HBM)

    kv_s, kv_give = call(
        pack_kv_kernel,
        "pack_kv",
        [shape(kv_block, low)] * 2,
        [pltpu.VMEM(key_rows.shape, low)] * 2
        + [pltpu.VMEM((rows, 2 * groups, size), f32), pltpu.SemaphoreType.DMA((2,))],
        in_specs=[hbm, hbm],
    )(pin(key_rows), pin(value_rows))
    kv_r = move(kv_give, sibling)
    two_s = move(kv_s, ahead)
    two_r = move(kv_r, ahead)
    q_s, g_s, rows_s, q_give, g_give = call(
        pack_q_kernel,
        "pack_q",
        [
            shape((half_rows, size), low),
            shape((half_rows, size), low),
            shape(row_block, f32),
            shape((half_rows + 3 * row_block[0], size), low),
            shape((half_rows, size), low),
        ],
        [pltpu.VMEM(queries.shape, low)] * 3
        + [pltpu.VMEM((rows, heads, size), f32), pltpu.VMEM(row_block, f32), pltpu.SemaphoreType.DMA((3,))],
        in_specs=[hbm, hbm, hbm, vmem, anywhere],
    )(pin(queries), pin(grad_output), pin(attn_output), log_norm, kv_r)
    q_r, g_r = move(q_give, sibling), move(g_give, sibling)
    acc = [shape(gq_block, f32)] * 2
    grad_scratch = [pltpu.VMEM(kv_block, f32)]
    two_s, rows_s = lax.optimization_barrier((two_s, rows_s))
    one_s = move(jnp.where(even, kv_s, two_s), beside)
    sides = (q_s, g_s, rows_s, q_r, g_r)
    grad_s, gq_s = call(own_side_kernel, "own_side", [shape(kv_block, f32), acc[0]], flops=0)(
        kv_s, q_s, g_s, rows_s
    )
    own_s, own_r, gq_s, gq_r = call(own_rest_kernel, "own_rest", [shape(kv_block, f32)] * 2 + acc, flops=0)(
        kv_s, kv_r, *sides, grad_s, gq_s
    )
    far_s, gq_s, gq_r = call(
        functools.partial(far_kernel, True), "far_s", [shape(kv_block, low)] + acc, grad_scratch
    )(two_s, *sides, gq_s, gq_r)
    back_s = move(far_s, behind)
    two_r, gq_s, gq_r = lax.optimization_barrier((two_r, gq_s, gq_r))
    one_r = move(jnp.where(even, kv_r, two_r), beside)
    far_r, gq_s, gq_r = call(
        functools.partial(far_kernel, False),
        "far_r",
        [shape(kv_block, low)] + acc,
        grad_scratch,
    )(two_r, *sides, gq_s, gq_r)
    back_r = move(far_r, lambda i: sibling(behind(i)))
    near = functools.partial(call, near_kernel, out_shape=[shape(kv_block, low)] + acc, scratch=grad_scratch)
    near_s, gq_s, gq_r = near(name="near_s")(one_s, *sides, gq_s, gq_r)
    side_s = move(near_s, lambda i: i - 2)
    back_s, one_r = lax.optimization_barrier((back_s, one_r))
    near_r, gq_s, gq_r = near(name="near_r")(one_r, *sides, gq_s, gq_r)
    side_r = move(near_r, lambda i: sibling(i - 2) if i >= 2 else -1)

    part = call(partial_kernel, "partial", shape(kv_block, f32), flops=LONG)(own_s, back_s)
    give = jnp.concatenate([own_r.astype(low), (gq_r * query_scale).astype(low).reshape(-1, rows, size)])
    got = move(give, sibling)
    grad_q, token = call(
        final_q_kernel,
        "final_q",
        [shape(queries.shape, low), shape((8, 128), f32)],
        [pltpu.VMEM((rows, heads, size), f32)],
        in_specs=[vmem, vmem, anywhere],
    )(gq_s, got, part)
    grad_k, grad_v = call(
        final_kv_kernel,
        "final_kv",
        [shape(key_rows.shape, low), shape(value_rows.shape, low)],
        [pltpu.VMEM((rows, 2 * groups, size), f32)],
        in_specs=[vmem] * 5 + [anywhere],
    )(part, got, back_r, side_s, side_r, token)
    return grad_q, grad_k, grad_v


def solution(mesh):
    in_specs = (
        P("seq", None, None),
        P("seq", None, None),
        P("seq", None, None),
        P("seq", None, None),
        P("seq", None, None),
        P(None, "seq"),
    )
    out_specs = (P("seq", None, None), P("seq", None, None), P("seq", None, None))
    return jax.shard_map(shards, mesh=mesh, in_specs=in_specs, out_specs=out_specs, check_vma=False)
```

```python
import functools
import math

import jax
import jax.numpy as jnp
from jax import lax
from jax.experimental import pallas as pl
from jax.experimental.pallas import tpu as pltpu
from jax.sharding import PartitionSpec as P

W = 1024

query_scale = 168.0 ** (-0.5)
LOG2E = math.log2(math.e)
AXIS = "seq"
VMEM_LIMIT = 16 * 1024 * 1024
LONG = 10**10

NT = (((1,), (1,)), ((), ()))
NN = (((1,), (0,)), ((), ()))
TN = (((0,), (0,)), ((), ()))


def dot(a, b, dims):
    return lax.dot_general(a, b, dims, preferred_element_type=jnp.float32)


def call(kernel, name, out_shape, scratch=(), flops=0, in_specs=None):
    specs = {} if in_specs is None else {"in_specs": in_specs}
    return pl.pallas_call(
        kernel,
        out_shape=out_shape,
        scratch_shapes=list(scratch),
        name=name,
        cost_estimate=pl.CostEstimate(flops=flops, bytes_accessed=2 << 20, transcendentals=0),
        compiler_params=pltpu.CompilerParams(vmem_limit_bytes=VMEM_LIMIT),
        **specs,
    )


def fetch(pairs, sems):
    copies = [pltpu.make_async_copy(src, dst, sems.at[n]) for n, (src, dst) in enumerate(pairs)]
    for copy in copies:
        copy.start()
    return copies


def pack_kv_kernel(k_hbm, v_hbm, keep_ref, give_ref, k_ref, v_ref, wide, sems):
    copy_k, copy_v = fetch(((k_hbm, k_ref), (v_hbm, v_ref)), sems)
    rows, heads, _ = k_ref.shape
    half = heads // 2
    core = lax.axis_index(AXIS) % 2
    copy_k.wait()
    wide[:, :heads, :] = k_ref[...].astype(jnp.float32)
    copy_v.wait()
    wide[:, heads:, :] = v_ref[...].astype(jnp.float32)
    flat = wide.reshape(rows * 2 * heads, wide.shape[2])
    for out, side in ((keep_ref, core), (give_ref, 1 - core)):
        for part in range(2):
            for j in range(half):
                head = part * heads + side * half + j
                out[part * half + j] = flat[pl.ds(head, rows, stride=2 * heads), :].astype(out.dtype)


def split_three(x):
    parts = []
    for _ in range(3):
        part = x.astype(jnp.bfloat16)
        parts.append(part)
        x = x - part.astype(jnp.float32)
    return parts


def join_three(ref, start, count):
    high, mid, low = (ref[start + n * count : start + (n + 1) * count].astype(jnp.float32) for n in range(3))
    return high + mid + low


def pack_q_kernel(
    q_hbm,
    g_hbm,
    o_hbm,
    norm_ref,
    after,
    keep_q,
    keep_g,
    keep_rows,
    give_q,
    give_g,
    q_ref,
    g_ref,
    o_ref,
    wide,
    give_rows,
    sems,
):
    copy_q, copy_g, copy_o = fetch(((q_hbm, q_ref), (g_hbm, g_ref), (o_hbm, o_ref)), sems)
    rows, heads, size = q_ref.shape
    half = heads // 2
    pieces = rows // size
    core = lax.axis_index(AXIS) % 2
    ones = jnp.ones((8, size), jnp.float32)
    flat = wide.reshape(rows * heads, size)

    def spread(outs):
        for out, side in zip(outs, (core, 1 - core), strict=True):
            for j in range(half):
                block = flat[pl.ds(side * half + j, rows, stride=heads), :]
                out[j * rows : (j + 1) * rows] = block.astype(out.dtype)

    copy_q.wait()
    wide[...] = q_ref[...].astype(jnp.float32)
    spread((keep_q, give_q))
    copy_g.wait()
    wide[...] = g_ref[...].astype(jnp.float32)
    spread((keep_g, give_g))
    copy_o.wait()
    wide[...] = g_ref[...].astype(jnp.float32) * o_ref[...].astype(jnp.float32)
    for out, side in ((keep_rows, core), (give_rows, 1 - core)):
        for j in range(half):
            product = flat[pl.ds(side * half + j, rows, stride=heads), :]
            delta = lax.dot_general(
                ones, product, NT, precision=lax.Precision.HIGHEST, preferred_element_type=jnp.float32
            )
            norm = norm_ref[pl.ds(side * half + j, 1), :] * LOG2E
            for n in range(pieces):
                out[j * pieces + n : j * pieces + n + 1] = norm[:, n * size : (n + 1) * size]
                at = (half + j) * pieces + n
                out[at : at + 1] = delta[:1, n * size : (n + 1) * size]
    count = heads * pieces
    for n, part in enumerate(split_three(give_rows[...])):
        give_q[half * rows + n * count : half * rows + (n + 1) * count] = part


def tile(kv_ref, side, grad_ref, gq_in, gq_ref, offset, first):
    q_ref, g_ref, row_ref = side
    groups = kv_ref.shape[0] // 2
    rows, size = kv_ref.shape[1], kv_ref.shape[2]
    span = gq_ref.shape[1]
    share = span // rows
    pieces = span // size
    if row_ref is None:
        vectors = join_three(q_ref, g_ref.shape[0], 2 * groups * pieces)
    else:
        vectors = row_ref[...]

    def vector(at):
        return jnp.concatenate([vectors[at + n : at + n + 1] for n in range(pieces)], 1)

    for g in range(groups):
        k = kv_ref[g]
        v = kv_ref[groups + g]
        q = q_ref[g * span : (g + 1) * span]
        d = g_ref[g * span : (g + 1) * span]
        norm = vector(g * pieces)
        delta = vector((groups + g) * pieces)
        x = dot(k, q, NT) * (query_scale * LOG2E) - norm
        if offset is not None:
            key = lax.broadcasted_iota(jnp.int32, (rows, rows), 0)
            query = lax.broadcasted_iota(jnp.int32, (rows, rows), 1)
            gap = query - key + offset
            seen = (gap >= 0) & (gap < W)
            x = jnp.concatenate(
                [jnp.where(seen, x[:, j * rows : (j + 1) * rows], -jnp.inf) for j in range(share)], 1
            )
        p = jnp.exp2(x)
        ds = (p * (dot(v, d, NT) - delta)).astype(jnp.bfloat16)
        gv = dot(p.astype(jnp.bfloat16), d, NN)
        gk = dot(ds, q, NN)
        gq = dot(ds, k, TN)
        if first:
            grad_ref[g] = gk
            grad_ref[groups + g] = gv
        else:
            grad_ref[g] += gk
            grad_ref[groups + g] += gv
        gq_ref[g] = gq if gq_in is None else gq_in[g] + gq


def scale_keys(grad_ref):
    groups = grad_ref.shape[0] // 2
    grad_ref[:groups] = grad_ref[:groups] * query_scale


def own_side_kernel(kv_s, q_s, g_s, rows_s, grad_s, gq_s):
    tile(kv_s, (q_s, g_s, rows_s), grad_s, None, gq_s, 0, True)


def own_rest_kernel(kv_s, kv_r, q_s, g_s, rows_s, q_r, g_r, grad_s_in, gq_s_in, grad_s, grad_r, gq_s, gq_r):
    side_s, side_r = (q_s, g_s, rows_s), (q_r, g_r, None)
    core = lax.axis_index(AXIS) % 2
    grad_s[...] = grad_s_in[...]
    tile(kv_r, side_r, grad_r, None, gq_r, 0, True)

    @pl.when(core == 0)
    def _():
        tile(kv_s, side_r, grad_s, gq_r, gq_r, None, False)
        gq_s[...] = gq_s_in[...]

    @pl.when(core == 1)
    def _():
        tile(kv_r, side_s, grad_r, gq_s_in, gq_s, None, False)

    scale_keys(grad_s)
    scale_keys(grad_r)


def far_kernel(first, kv, q_s, g_s, rows_s, q_r, g_r, *refs):
    if first:
        gq_s_in, gq_r_in, out, gq_s, gq_r, grad = refs
        side_s, side_r, seen_by = (q_s, g_s, rows_s), (q_r, g_r, None), 1
    else:
        gq_r_in, gq_s_in, out, gq_r, gq_s, grad = refs
        side_s, side_r, seen_by = (q_r, g_r, None), (q_s, g_s, rows_s), 0
    device = lax.axis_index(AXIS)
    core = device % 2
    valid = device // 2 >= 2

    @pl.when(valid)
    def _():
        tile(kv, side_s, grad, gq_s_in, gq_s, W, True)

    @pl.when(valid & (core == seen_by))
    def _():
        tile(kv, side_r, grad, gq_r_in, gq_r, None, False)

    @pl.when(valid)
    def _():
        scale_keys(grad)
        out[...] = grad[...].astype(out.dtype)

    @pl.when(jnp.logical_not(valid))
    def _():
        out[...] = jnp.zeros_like(out)
        gq_s[...] = gq_s_in[...]

    @pl.when(jnp.logical_not(valid & (core == seen_by)))
    def _():
        gq_r[...] = gq_r_in[...]


def near_kernel(kv, q_s, g_s, rows_s, q_r, g_r, gq_s_in, gq_r_in, out, gq_s, gq_r, grad):
    side_s, side_r = (q_s, g_s, rows_s), (q_r, g_r, None)
    valid = lax.axis_index(AXIS) // 2 >= 1

    @pl.when(valid)
    def _():
        tile(kv, side_s, grad, gq_s_in, gq_s, None, True)
        tile(kv, side_r, grad, gq_r_in, gq_r, None, False)
        scale_keys(grad)
        out[...] = grad[...].astype(out.dtype)

    @pl.when(jnp.logical_not(valid))
    def _():
        out[...] = jnp.zeros_like(out)
        gq_s[...] = gq_s_in[...]
        gq_r[...] = gq_r_in[...]


def final_q_kernel(own_ref, got_ref, after, out_ref, token_ref, wide):
    token_ref[...] = jnp.zeros_like(token_ref)
    rows, heads, size = out_ref.shape
    half = heads // 2
    core = lax.axis_index(AXIS) % 2
    flat = wide.reshape(rows * heads, size)
    share = half // own_ref.shape[0]
    skip = got_ref.shape[0] - half
    for j in range(half):
        g, r = j // share, j % share
        flat[pl.ds(core * half + j, rows, stride=heads), :] = own_ref[g, r * rows : (r + 1) * rows] * query_scale
        flat[pl.ds((1 - core) * half + j, rows, stride=heads), :] = got_ref[skip + j].astype(jnp.float32)
    out_ref[...] = wide[...].astype(out_ref.dtype)


def partial_kernel(own_ref, back_ref, out_ref):
    out_ref[...] = own_ref[...] + back_ref[...].astype(jnp.float32)


def final_kv_kernel(part_ref, got_ref, back_r, side_s, side_r, after, out_k, out_v, wide):
    rows, heads, size = out_k.shape
    half = heads // 2
    core = lax.axis_index(AXIS) % 2
    flat = wide.reshape(rows * 2 * heads, size)
    for part in range(2):
        for j in range(half):
            n = part * half + j
            flat[pl.ds(part * heads + core * half + j, rows, stride=2 * heads), :] = part_ref[n] + side_s[n].astype(
                jnp.float32
            )
            flat[pl.ds(part * heads + (1 - core) * half + j, rows, stride=2 * heads), :] = (
                got_ref[n].astype(jnp.float32)
                + back_r[n].astype(jnp.float32)
                + side_r[n].astype(jnp.float32)
            )
    out_k[...] = wide[:, :heads, :].astype(out_k.dtype)
    out_v[...] = wide[:, heads:, :].astype(out_v.dtype)


def shards(queries, key_rows, value_rows, attn_output, grad_output, log_norm):
    rows, heads, size = queries.shape
    groups = key_rows.shape[1]
    devices = lax.axis_size(AXIS)
    hops = W // rows
    assert hops == 4 and devices % 4 == 0
    low, f32 = jnp.bfloat16, jnp.float32
    device = lax.axis_index(AXIS)
    even = (device // 2) % 2 == 0

    def move(x, target):
        pairs = [(i, target(i)) for i in range(devices)]
        return lax.ppermute(x, AXIS, [(i, j) for i, j in pairs if j >= 0])

    ahead = lambda i: (i + hops) % devices
    behind = lambda i: (i - hops) % devices
    sibling = lambda i: i ^ 1
    beside = lambda i: i ^ 2

    shape = jax.ShapeDtypeStruct
    kv_block = (groups, rows, size)
    half_rows = heads * rows // 2
    row_block = (heads * rows // size, size)
    gq_block = (groups // 2, heads // groups * rows, size)

    hbm = pl.BlockSpec(memory_space=pltpu.HBM)
    vmem = pl.BlockSpec(memory_space=pltpu.VMEM)
    anywhere = pl.BlockSpec(memory_space=pl.ANY)
    hbm = pl.BlockSpec(memory_space=pltpu.HBM)
    vmem = pl.BlockSpec(memory_space=pltpu.VMEM)
    anywhere = pl.BlockSpec(memory_space=pl.ANY)

    def pin(x):
        return pltpu.with_memory_space_constraint(x, pltpu.HBM)

    kv_s, kv_give = call(
        pack_kv_kernel,
        "pack_kv",
        [shape(kv_block, low)] * 2,
        [pltpu.VMEM(key_rows.shape, low)] * 2
        + [pltpu.VMEM((rows, 2 * groups, size), f32), pltpu.SemaphoreType.DMA((2,))],
        in_specs=[hbm, hbm],
    )(pin(key_rows), pin(value_rows))
    kv_r = move(kv_give, sibling)
    two_s = move(kv_s, ahead)
    two_r = move(kv_r, ahead)
    q_s, g_s, rows_s, q_give, g_give = call(
        pack_q_kernel,
        "pack_q",
        [
            shape((half_rows, size), low),
            shape((half_rows, size), low),
            shape(row_block, f32),
            shape((half_rows + 3 * row_block[0], size), low),
            shape((half_rows, size), low),
        ],
        [pltpu.VMEM(queries.shape, low)] * 3
        + [pltpu.VMEM((rows, heads, size), f32), pltpu.VMEM(row_block, f32), pltpu.SemaphoreType.DMA((3,))],
        in_specs=[hbm, hbm, hbm, vmem, anywhere],
    )(pin(queries), pin(grad_output), pin(attn_output), log_norm, kv_r)
    q_r, g_r = move(q_give, sibling), move(g_give, sibling)
    acc = [shape(gq_block, f32)] * 2
    grad_scratch = [pltpu.VMEM(kv_block, f32)]
    grad_s, gq_s = call(own_side_kernel, "own_side", [shape(kv_block, f32), acc[0]], flops=0)(
        kv_s, q_s, g_s, rows_s
    )
    two_s, grad_s = lax.optimization_barrier((two_s, grad_s))
    one_s = move(jnp.where(even, kv_s, two_s), beside)
    sides = (q_s, g_s, rows_s, q_r, g_r)
    own_s, own_r, gq_s, gq_r = call(own_rest_kernel, "own_rest", [shape(kv_block, f32)] * 2 + acc, flops=0)(
        kv_s, kv_r, *sides, grad_s, gq_s
    )
    far_s, gq_s, gq_r = call(
        functools.partial(far_kernel, True), "far_s", [shape(kv_block, low)] + acc, grad_scratch
    )(two_s, *sides, gq_s, gq_r)
    back_s = move(far_s, behind)
    two_r, gq_s, gq_r = lax.optimization_barrier((two_r, gq_s, gq_r))
    one_r = move(jnp.where(even, kv_r, two_r), beside)
    far_r, gq_s, gq_r = call(
        functools.partial(far_kernel, False),
        "far_r",
        [shape(kv_block, low)] + acc,
        grad_scratch,
    )(two_r, *sides, gq_s, gq_r)
    back_r = move(far_r, lambda i: sibling(behind(i)))
    near = functools.partial(call, near_kernel, out_shape=[shape(kv_block, low)] + acc, scratch=grad_scratch)
    near_s, gq_s, gq_r = near(name="near_s")(one_s, *sides, gq_s, gq_r)
    side_s = move(near_s, lambda i: i - 2)
    back_s, one_r = lax.optimization_barrier((back_s, one_r))
    near_r, gq_s, gq_r = near(name="near_r")(one_r, *sides, gq_s, gq_r)
    side_r = move(near_r, lambda i: sibling(i - 2) if i >= 2 else -1)

    part = call(partial_kernel, "partial", shape(kv_block, f32), flops=LONG)(own_s, back_s)
    give = jnp.concatenate([own_r.astype(low), (gq_r * query_scale).astype(low).reshape(-1, rows, size)])
    got = move(give, sibling)
    grad_q, token = call(
        final_q_kernel,
        "final_q",
        [shape(queries.shape, low), shape((8, 128), f32)],
        [pltpu.VMEM((rows, heads, size), f32)],
        in_specs=[vmem, vmem, anywhere],
    )(gq_s, got, part)
    grad_k, grad_v = call(
        final_kv_kernel,
        "final_kv",
        [shape(key_rows.shape, low), shape(value_rows.shape, low)],
        [pltpu.VMEM((rows, 2 * groups, size), f32)],
        in_specs=[vmem] * 5 + [anywhere],
    )(part, got, back_r, side_s, side_r, token)
    return grad_q, grad_k, grad_v


def solution(mesh):
    in_specs = (
        P("seq", None, None),
        P("seq", None, None),
        P("seq", None, None),
        P("seq", None, None),
        P("seq", None, None),
        P(None, "seq"),
    )
    out_specs = (P("seq", None, None), P("seq", None, None), P("seq", None, None))
    return jax.shard_map(shards, mesh=mesh, in_specs=in_specs, out_specs=out_specs, check_vma=False)
```

```python
import functools
import math

import jax
import jax.numpy as jnp
from jax import lax
from jax.experimental import pallas as pl
from jax.experimental.pallas import tpu as pltpu
from jax.sharding import PartitionSpec as P

W = 1024

query_scale = 168.0 ** (-0.5)
LOG2E = math.log2(math.e)
AXIS = "seq"
VMEM_LIMIT = 16 * 1024 * 1024
LONG = 10**10

NT = (((1,), (1,)), ((), ()))
NN = (((1,), (0,)), ((), ()))
TN = (((0,), (0,)), ((), ()))


def dot(a, b, dims):
    return lax.dot_general(a, b, dims, preferred_element_type=jnp.float32)


def call(kernel, name, out_shape, scratch=(), flops=0, in_specs=None):
    specs = {} if in_specs is None else {"in_specs": in_specs}
    return pl.pallas_call(
        kernel,
        out_shape=out_shape,
        scratch_shapes=list(scratch),
        name=name,
        cost_estimate=pl.CostEstimate(flops=flops, bytes_accessed=2 << 20, transcendentals=0),
        compiler_params=pltpu.CompilerParams(vmem_limit_bytes=VMEM_LIMIT),
        **specs,
    )


def fetch(pairs, sems):
    copies = [pltpu.make_async_copy(src, dst, sems.at[n]) for n, (src, dst) in enumerate(pairs)]
    for copy in copies:
        copy.start()
    return copies


def pack_kv_kernel(k_hbm, v_hbm, keep_ref, give_ref, k_ref, v_ref, wide, sems):
    copy_k, copy_v = fetch(((k_hbm, k_ref), (v_hbm, v_ref)), sems)
    rows, heads, _ = k_ref.shape
    half = heads // 2
    core = lax.axis_index(AXIS) % 2
    copy_k.wait()
    wide[:, :heads, :] = k_ref[...].astype(jnp.float32)
    copy_v.wait()
    wide[:, heads:, :] = v_ref[...].astype(jnp.float32)
    flat = wide.reshape(rows * 2 * heads, wide.shape[2])
    for out, side in ((keep_ref, core), (give_ref, 1 - core)):
        for part in range(2):
            for j in range(half):
                head = part * heads + side * half + j
                out[part * half + j] = flat[pl.ds(head, rows, stride=2 * heads), :].astype(out.dtype)


def split_three(x):
    parts = []
    for _ in range(3):
        part = x.astype(jnp.bfloat16)
        parts.append(part)
        x = x - part.astype(jnp.float32)
    return parts


def join_three(ref, start, count):
    high, mid, low = (ref[start + n * count : start + (n + 1) * count].astype(jnp.float32) for n in range(3))
    return high + mid + low


def pack_q_kernel(
    q_hbm,
    g_hbm,
    o_hbm,
    norm_ref,
    after,
    keep_q,
    keep_g,
    keep_rows,
    give_q0,
    give_q1,
    give_g0,
    give_g1,
    q_ref,
    g_ref,
    o_ref,
    wide,
    give_rows,
    sems,
):
    copy_q, copy_g, copy_o = fetch(((q_hbm, q_ref), (g_hbm, g_ref), (o_hbm, o_ref)), sems)
    rows, heads, size = q_ref.shape
    half = heads // 2
    pieces = rows // size
    core = lax.axis_index(AXIS) % 2
    ones = jnp.ones((16, size), jnp.bfloat16)
    flat = wide.reshape(rows * heads, size)

    def spread(outs):
        keep, low, high = outs
        for j in range(half):
            block = flat[pl.ds(core * half + j, rows, stride=heads), :]
            keep[j * rows : (j + 1) * rows] = block.astype(keep.dtype)
            block = flat[pl.ds((1 - core) * half + j, rows, stride=heads), :]
            out, at = (low, j) if j < half // 2 else (high, j - half // 2)
            out[at * rows : (at + 1) * rows] = block.astype(out.dtype)

    copy_q.wait()
    wide[...] = q_ref[...].astype(jnp.float32)
    spread((keep_q, give_q0, give_q1))
    copy_g.wait()
    wide[...] = g_ref[...].astype(jnp.float32)
    spread((keep_g, give_g0, give_g1))
    copy_o.wait()
    wide[...] = g_ref[...].astype(jnp.float32) * o_ref[...].astype(jnp.float32)
    for out, side in ((keep_rows, core), (give_rows, 1 - core)):
        for j in range(half):
            product = flat[pl.ds(side * half + j, rows, stride=heads), :]
            high = product.astype(jnp.bfloat16)
            rest = (product - high.astype(jnp.float32)).astype(jnp.bfloat16)
            delta = dot(ones, high, NT) + dot(ones, rest, NT)
            norm = norm_ref[pl.ds(side * half + j, 1), :] * LOG2E
            for n in range(pieces):
                out[j * pieces + n : j * pieces + n + 1] = norm[:, n * size : (n + 1) * size]
                at = (half + j) * pieces + n
                out[at : at + 1] = delta[:1, n * size : (n + 1) * size]
    count = heads * pieces
    for n, part in enumerate(split_three(give_rows[...])):
        start = half // 2 * rows + n * count
        give_q0[start : start + count] = part


def tile(kv_ref, side, grad_ref, gq_in, gq_ref, offset, first):
    q_ref, g_ref, row_ref = side
    groups = kv_ref.shape[0] // 2
    rows, size = kv_ref.shape[1], kv_ref.shape[2]
    span = gq_ref.shape[1]
    share = span // rows
    pieces = span // size
    if row_ref is None:
        vectors = join_three(q_ref[0], g_ref[0].shape[0], 2 * groups * pieces)
    else:
        vectors = row_ref[...]

    def vector(at):
        return jnp.concatenate([vectors[at + n : at + n + 1] for n in range(pieces)], 1)

    for g in range(groups):
        k = kv_ref[g]
        v = kv_ref[groups + g]
        if row_ref is None:
            q, d = q_ref[g][:span], g_ref[g][...]
        else:
            q = q_ref[g * span : (g + 1) * span]
            d = g_ref[g * span : (g + 1) * span]
        norm = vector(g * pieces)
        delta = vector((groups + g) * pieces)
        x = dot(k, q, NT) * (query_scale * LOG2E) - norm
        if offset is not None:
            key = lax.broadcasted_iota(jnp.int32, (rows, rows), 0)
            query = lax.broadcasted_iota(jnp.int32, (rows, rows), 1)
            gap = query - key + offset
            seen = (gap >= 0) & (gap < W)
            x = jnp.concatenate(
                [jnp.where(seen, x[:, j * rows : (j + 1) * rows], -jnp.inf) for j in range(share)], 1
            )
        p = jnp.exp2(x)
        ds = (p * (dot(v, d, NT) - delta)).astype(jnp.bfloat16)
        gv = dot(p.astype(jnp.bfloat16), d, NN)
        gk = dot(ds, q, NN)
        gq = dot(ds, k, TN)
        if first:
            grad_ref[g] = gk
            grad_ref[groups + g] = gv
        else:
            grad_ref[g] += gk
            grad_ref[groups + g] += gv
        gq_ref[g] = gq if gq_in is None else gq_in[g] + gq


def scale_keys(grad_ref):
    groups = grad_ref.shape[0] // 2
    grad_ref[:groups] = grad_ref[:groups] * query_scale


def own_side_kernel(kv_s, q_s, g_s, rows_s, grad_s, gq_s):
    tile(kv_s, (q_s, g_s, rows_s), grad_s, None, gq_s, 0, True)


def own_rest_kernel(kv_s, kv_r, q_s, g_s, rows_s, q_r0, q_r1, g_r0, g_r1, grad_s_in, gq_s_in, grad_s, grad_r, gq_s, gq_r):
    side_s, side_r = (q_s, g_s, rows_s), ((q_r0, q_r1), (g_r0, g_r1), None)
    core = lax.axis_index(AXIS) % 2
    grad_s[...] = grad_s_in[...]
    tile(kv_r, side_r, grad_r, None, gq_r, 0, True)

    @pl.when(core == 0)
    def _():
        tile(kv_s, side_r, grad_s, gq_r, gq_r, None, False)
        gq_s[...] = gq_s_in[...]

    @pl.when(core == 1)
    def _():
        tile(kv_r, side_s, grad_r, gq_s_in, gq_s, None, False)

    scale_keys(grad_s)
    scale_keys(grad_r)


def far_kernel(first, kv, q_s, g_s, rows_s, q_r0, q_r1, g_r0, g_r1, *refs):
    if first:
        gq_s_in, gq_r_in, out, gq_s, gq_r, grad = refs
        side_s, side_r, seen_by = (q_s, g_s, rows_s), ((q_r0, q_r1), (g_r0, g_r1), None), 1
    else:
        gq_r_in, gq_s_in, out, gq_r, gq_s, grad = refs
        side_s, side_r, seen_by = ((q_r0, q_r1), (g_r0, g_r1), None), (q_s, g_s, rows_s), 0
    device = lax.axis_index(AXIS)
    core = device % 2
    valid = device // 2 >= 2

    @pl.when(valid)
    def _():
        tile(kv, side_s, grad, gq_s_in, gq_s, W, True)

    @pl.when(valid & (core == seen_by))
    def _():
        tile(kv, side_r, grad, gq_r_in, gq_r, None, False)

    @pl.when(valid)
    def _():
        scale_keys(grad)
        out[...] = grad[...].astype(out.dtype)

    @pl.when(jnp.logical_not(valid))
    def _():
        out[...] = jnp.zeros_like(out)
        gq_s[...] = gq_s_in[...]

    @pl.when(jnp.logical_not(valid & (core == seen_by)))
    def _():
        gq_r[...] = gq_r_in[...]


def near_kernel(kv, q_s, g_s, rows_s, q_r0, q_r1, g_r0, g_r1, gq_s_in, gq_r_in, out, gq_s, gq_r, grad):
    side_s, side_r = (q_s, g_s, rows_s), ((q_r0, q_r1), (g_r0, g_r1), None)
    valid = lax.axis_index(AXIS) // 2 >= 1

    @pl.when(valid)
    def _():
        tile(kv, side_s, grad, gq_s_in, gq_s, None, True)
        tile(kv, side_r, grad, gq_r_in, gq_r, None, False)
        scale_keys(grad)
        out[...] = grad[...].astype(out.dtype)

    @pl.when(jnp.logical_not(valid))
    def _():
        out[...] = jnp.zeros_like(out)
        gq_s[...] = gq_s_in[...]
        gq_r[...] = gq_r_in[...]


def final_q_kernel(own_ref, got_ref, after, out_ref, token_ref, wide):
    token_ref[...] = jnp.zeros_like(token_ref)
    rows, heads, size = out_ref.shape
    half = heads // 2
    core = lax.axis_index(AXIS) % 2
    flat = wide.reshape(rows * heads, size)
    share = half // own_ref.shape[0]
    skip = got_ref.shape[0] - half
    for j in range(half):
        g, r = j // share, j % share
        flat[pl.ds(core * half + j, rows, stride=heads), :] = own_ref[g, r * rows : (r + 1) * rows] * query_scale
        flat[pl.ds((1 - core) * half + j, rows, stride=heads), :] = got_ref[skip + j].astype(jnp.float32)
    out_ref[...] = wide[...].astype(out_ref.dtype)


def partial_kernel(own_ref, back_ref, out_ref):
    out_ref[...] = own_ref[...] + back_ref[...].astype(jnp.float32)


def final_kv_kernel(part_ref, got_ref, back_r, side_s, side_r, after, out_k, out_v, wide):
    rows, heads, size = out_k.shape
    half = heads // 2
    core = lax.axis_index(AXIS) % 2
    flat = wide.reshape(rows * 2 * heads, size)
    for part in range(2):
        for j in range(half):
            n = part * half + j
            flat[pl.ds(part * heads + core * half + j, rows, stride=2 * heads), :] = part_ref[n] + side_s[n].astype(
                jnp.float32
            )
            flat[pl.ds(part * heads + (1 - core) * half + j, rows, stride=2 * heads), :] = (
                got_ref[n].astype(jnp.float32)
                + back_r[n].astype(jnp.float32)
                + side_r[n].astype(jnp.float32)
            )
    out_k[...] = wide[:, :heads, :].astype(out_k.dtype)
    out_v[...] = wide[:, heads:, :].astype(out_v.dtype)


def shards(queries, key_rows, value_rows, attn_output, grad_output, log_norm):
    rows, heads, size = queries.shape
    groups = key_rows.shape[1]
    devices = lax.axis_size(AXIS)
    hops = W // rows
    assert hops == 4 and devices % 4 == 0
    low, f32 = jnp.bfloat16, jnp.float32
    device = lax.axis_index(AXIS)
    even = (device // 2) % 2 == 0

    def move(x, target):
        pairs = [(i, target(i)) for i in range(devices)]
        return lax.ppermute(x, AXIS, [(i, j) for i, j in pairs if j >= 0])

    ahead = lambda i: (i + hops) % devices
    behind = lambda i: (i - hops) % devices
    sibling = lambda i: i ^ 1
    beside = lambda i: i ^ 2

    shape = jax.ShapeDtypeStruct
    kv_block = (groups, rows, size)
    half_rows = heads * rows // 2
    row_block = (heads * rows // size, size)
    gq_block = (groups // 2, heads // groups * rows, size)

    hbm = pl.BlockSpec(memory_space=pltpu.HBM)
    vmem = pl.BlockSpec(memory_space=pltpu.VMEM)
    anywhere = pl.BlockSpec(memory_space=pl.ANY)
    hbm = pl.BlockSpec(memory_space=pltpu.HBM)
    vmem = pl.BlockSpec(memory_space=pltpu.VMEM)
    anywhere = pl.BlockSpec(memory_space=pl.ANY)

    def pin(x):
        return pltpu.with_memory_space_constraint(x, pltpu.HBM)

    kv_s, kv_give = call(
        pack_kv_kernel,
        "pack_kv",
        [shape(kv_block, low)] * 2,
        [pltpu.VMEM(key_rows.shape, low)] * 2
        + [pltpu.VMEM((rows, 2 * groups, size), f32), pltpu.SemaphoreType.DMA((2,))],
        in_specs=[hbm, hbm],
    )(pin(key_rows), pin(value_rows))
    kv_r = move(kv_give, sibling)
    two_s = move(kv_s, ahead)
    two_r = move(kv_r, ahead)
    q_s, g_s, rows_s, *gives = call(
        pack_q_kernel,
        "pack_q",
        [
            shape((half_rows, size), low),
            shape((half_rows, size), low),
            shape(row_block, f32),
            shape((half_rows // 2 + 3 * row_block[0], size), low),
            shape((half_rows // 2, size), low),
            shape((half_rows // 2, size), low),
            shape((half_rows // 2, size), low),
        ],
        [pltpu.VMEM(queries.shape, low)] * 3
        + [pltpu.VMEM((rows, heads, size), f32), pltpu.VMEM(row_block, f32), pltpu.SemaphoreType.DMA((3,))],
        in_specs=[hbm, hbm, hbm, vmem, anywhere],
    )(pin(queries), pin(grad_output), pin(attn_output), log_norm, kv_r)
    received = [move(x, sibling) for x in gives]
    acc = [shape(gq_block, f32)] * 2
    grad_scratch = [pltpu.VMEM(kv_block, f32)]
    grad_s, gq_s = call(own_side_kernel, "own_side", [shape(kv_block, f32), acc[0]], flops=0)(
        kv_s, q_s, g_s, rows_s
    )
    sides = (q_s, g_s, rows_s, *received)
    own_s, own_r, gq_s, gq_r = call(own_rest_kernel, "own_rest", [shape(kv_block, f32)] * 2 + acc, flops=0)(
        kv_s, kv_r, *sides, grad_s, gq_s
    )
    two_s, gq_s, gq_r = lax.optimization_barrier((two_s, gq_s, gq_r))
    send_s = jnp.where(even, kv_s, two_s)
    one_s = move(send_s, beside)
    gq_s, gq_r, send_s = lax.optimization_barrier((gq_s, gq_r, send_s))
    far_s, gq_s, gq_r = call(
        functools.partial(far_kernel, True), "far_s", [shape(kv_block, low)] + acc, grad_scratch
    )(two_s, *sides, gq_s, gq_r)
    back_s = move(far_s, behind)
    two_r, gq_s, gq_r = lax.optimization_barrier((two_r, gq_s, gq_r))
    one_r = move(jnp.where(even, kv_r, two_r), beside)
    far_r, gq_s, gq_r = call(
        functools.partial(far_kernel, False),
        "far_r",
        [shape(kv_block, low)] + acc,
        grad_scratch,
    )(two_r, *sides, gq_s, gq_r)
    back_r = move(far_r, lambda i: sibling(behind(i)))
    near = functools.partial(call, near_kernel, out_shape=[shape(kv_block, low)] + acc, scratch=grad_scratch)
    near_s, gq_s, gq_r = near(name="near_s")(one_s, *sides, gq_s, gq_r)
    side_s = move(near_s, lambda i: i - 2)
    back_s, one_r = lax.optimization_barrier((back_s, one_r))
    near_r, gq_s, gq_r = near(name="near_r")(one_r, *sides, gq_s, gq_r)
    side_r = move(near_r, lambda i: sibling(i - 2) if i >= 2 else -1)

    part = call(partial_kernel, "partial", shape(kv_block, f32), flops=LONG)(own_s, back_s)
    give = jnp.concatenate([own_r.astype(low), (gq_r * query_scale).astype(low).reshape(-1, rows, size)])
    got = move(give, sibling)
    grad_q, token = call(
        final_q_kernel,
        "final_q",
        [shape(queries.shape, low), shape((8, 128), f32)],
        [pltpu.VMEM((rows, heads, size), f32)],
        in_specs=[vmem, vmem, anywhere],
    )(gq_s, got, part)
    grad_k, grad_v = call(
        final_kv_kernel,
        "final_kv",
        [shape(key_rows.shape, low), shape(value_rows.shape, low)],
        [pltpu.VMEM((rows, 2 * groups, size), f32)],
        in_specs=[vmem] * 5 + [anywhere],
    )(part, got, back_r, side_s, side_r, token)
    return grad_q, grad_k, grad_v


def solution(mesh):
    in_specs = (
        P("seq", None, None),
        P("seq", None, None),
        P("seq", None, None),
        P("seq", None, None),
        P("seq", None, None),
        P(None, "seq"),
    )
    out_specs = (P("seq", None, None), P("seq", None, None), P("seq", None, None))
    return jax.shard_map(shards, mesh=mesh, in_specs=in_specs, out_specs=out_specs, check_vma=False)
```

```python
import functools
import math

import jax
import jax.numpy as jnp
from jax import lax
from jax.experimental import pallas as pl
from jax.experimental.pallas import tpu as pltpu
from jax.sharding import PartitionSpec as P

W = 1024

query_scale = 168.0 ** (-0.5)
LOG2E = math.log2(math.e)
AXIS = "seq"
VMEM_LIMIT = 16 * 1024 * 1024
LONG = 10**10

NT = (((1,), (1,)), ((), ()))
NN = (((1,), (0,)), ((), ()))
TN = (((0,), (0,)), ((), ()))


def dot(a, b, dims):
    return lax.dot_general(a, b, dims, preferred_element_type=jnp.float32)


def call(kernel, name, out_shape, scratch=(), flops=0, in_specs=None):
    specs = {} if in_specs is None else {"in_specs": in_specs}
    return pl.pallas_call(
        kernel,
        out_shape=out_shape,
        scratch_shapes=list(scratch),
        name=name,
        cost_estimate=pl.CostEstimate(flops=flops, bytes_accessed=2 << 20, transcendentals=0),
        compiler_params=pltpu.CompilerParams(vmem_limit_bytes=VMEM_LIMIT),
        **specs,
    )


def fetch(pairs, sems):
    copies = [pltpu.make_async_copy(src, dst, sems.at[n]) for n, (src, dst) in enumerate(pairs)]
    for copy in copies:
        copy.start()
    return copies


def pack_kv_kernel(k_hbm, v_hbm, keep_ref, give_ref, k_ref, v_ref, wide, sems):
    copy_k, copy_v = fetch(((k_hbm, k_ref), (v_hbm, v_ref)), sems)
    rows, heads, _ = k_ref.shape
    half = heads // 2
    core = lax.axis_index(AXIS) % 2
    copy_k.wait()
    wide[:, :heads, :] = k_ref[...].astype(jnp.float32)
    copy_v.wait()
    wide[:, heads:, :] = v_ref[...].astype(jnp.float32)
    flat = wide.reshape(rows * 2 * heads, wide.shape[2])
    for out, side in ((keep_ref, core), (give_ref, 1 - core)):
        for part in range(2):
            for j in range(half):
                head = part * heads + side * half + j
                out[part * half + j] = flat[pl.ds(head, rows, stride=2 * heads), :].astype(out.dtype)


def split_three(x):
    parts = []
    for _ in range(3):
        part = x.astype(jnp.bfloat16)
        parts.append(part)
        x = x - part.astype(jnp.float32)
    return parts


def join_three(ref, start, count):
    high, mid, low = (ref[start + n * count : start + (n + 1) * count].astype(jnp.float32) for n in range(3))
    return high + mid + low


def pack_q_kernel(
    q_hbm,
    g_hbm,
    o_hbm,
    norm_ref,
    after,
    keep_q,
    keep_g,
    keep_rows,
    give_q0,
    give_q1,
    give_g0,
    give_g1,
    q_ref,
    g_ref,
    o_ref,
    wide,
    give_rows,
    sems,
):
    copy_q, copy_g, copy_o = fetch(((q_hbm, q_ref), (g_hbm, g_ref), (o_hbm, o_ref)), sems)
    rows, heads, size = q_ref.shape
    half = heads // 2
    pieces = rows // size
    core = lax.axis_index(AXIS) % 2
    ones = jnp.ones((16, size), jnp.bfloat16)
    flat = wide.reshape(rows * heads, size)

    def spread(outs):
        keep, low, high = outs
        for j in range(half):
            block = flat[pl.ds(core * half + j, rows, stride=heads), :]
            keep[j * rows : (j + 1) * rows] = block.astype(keep.dtype)
            block = flat[pl.ds((1 - core) * half + j, rows, stride=heads), :]
            out, at = (low, j) if j < half // 2 else (high, j - half // 2)
            out[at * rows : (at + 1) * rows] = block.astype(out.dtype)

    copy_q.wait()
    wide[...] = q_ref[...].astype(jnp.float32)
    spread((keep_q, give_q0, give_q1))
    copy_g.wait()
    wide[...] = g_ref[...].astype(jnp.float32)
    spread((keep_g, give_g0, give_g1))
    copy_o.wait()
    wide[...] = g_ref[...].astype(jnp.float32) * o_ref[...].astype(jnp.float32)
    for out, side in ((keep_rows, core), (give_rows, 1 - core)):
        for j in range(half):
            product = flat[pl.ds(side * half + j, rows, stride=heads), :]
            high = product.astype(jnp.bfloat16)
            rest = (product - high.astype(jnp.float32)).astype(jnp.bfloat16)
            delta = dot(ones, high, NT) + dot(ones, rest, NT)
            norm = norm_ref[pl.ds(side * half + j, 1), :] * LOG2E
            for n in range(pieces):
                out[j * pieces + n : j * pieces + n + 1] = norm[:, n * size : (n + 1) * size]
                at = (half + j) * pieces + n
                out[at : at + 1] = delta[:1, n * size : (n + 1) * size]
    count = heads * pieces
    for n, part in enumerate(split_three(give_rows[...])):
        start = half // 2 * rows + n * count
        give_q0[start : start + count] = part


def tile(kv_ref, side, grad_ref, gq_in, gq_ref, offset, first):
    q_ref, g_ref, row_ref = side
    groups = kv_ref.shape[0] // 2
    rows, size = kv_ref.shape[1], kv_ref.shape[2]
    span = gq_ref.shape[1]
    share = span // rows
    pieces = span // size
    if row_ref is None:
        vectors = join_three(q_ref[0], g_ref[0].shape[0], 2 * groups * pieces)
    else:
        vectors = row_ref[...]

    def vector(at):
        return jnp.concatenate([vectors[at + n : at + n + 1] for n in range(pieces)], 1)

    for g in range(groups):
        k = kv_ref[g]
        v = kv_ref[groups + g]
        if row_ref is None:
            q, d = q_ref[g][:span], g_ref[g][...]
        else:
            q = q_ref[g * span : (g + 1) * span]
            d = g_ref[g * span : (g + 1) * span]
        norm = vector(g * pieces)
        delta = vector((groups + g) * pieces)
        x = dot(k, q, NT) * (query_scale * LOG2E) - norm
        if offset is not None:
            key = lax.broadcasted_iota(jnp.int32, (rows, rows), 0)
            query = lax.broadcasted_iota(jnp.int32, (rows, rows), 1)
            gap = query - key + offset
            seen = (gap >= 0) & (gap < W)
            x = jnp.concatenate(
                [jnp.where(seen, x[:, j * rows : (j + 1) * rows], -jnp.inf) for j in range(share)], 1
            )
        p = jnp.exp2(x)
        ds = (p * (dot(v, d, NT) - delta)).astype(jnp.bfloat16)
        gv = dot(p.astype(jnp.bfloat16), d, NN)
        gk = dot(ds, q, NN)
        gq = dot(ds, k, TN)
        if first:
            grad_ref[g] = gk
            grad_ref[groups + g] = gv
        else:
            grad_ref[g] += gk
            grad_ref[groups + g] += gv
        gq_ref[g] = gq if gq_in is None else gq_in[g] + gq


def scale_keys(grad_ref):
    groups = grad_ref.shape[0] // 2
    grad_ref[:groups] = grad_ref[:groups] * query_scale


def own_side_kernel(kv_s, q_s, g_s, rows_s, grad_s, gq_s):
    tile(kv_s, (q_s, g_s, rows_s), grad_s, None, gq_s, 0, True)


def own_rest_kernel(kv_s, kv_r, q_s, g_s, rows_s, q_r0, q_r1, g_r0, g_r1, grad_s_in, gq_s_in, grad_s, grad_r, gq_s, gq_r):
    side_s, side_r = (q_s, g_s, rows_s), ((q_r0, q_r1), (g_r0, g_r1), None)
    core = lax.axis_index(AXIS) % 2
    grad_s[...] = grad_s_in[...]
    tile(kv_r, side_r, grad_r, None, gq_r, 0, True)

    @pl.when(core == 0)
    def _():
        tile(kv_s, side_r, grad_s, gq_r, gq_r, None, False)
        gq_s[...] = gq_s_in[...]

    @pl.when(core == 1)
    def _():
        tile(kv_r, side_s, grad_r, gq_s_in, gq_s, None, False)

    scale_keys(grad_s)
    scale_keys(grad_r)


def far_kernel(first, kv, q_s, g_s, rows_s, q_r0, q_r1, g_r0, g_r1, *refs):
    if first:
        gq_s_in, gq_r_in, out, gq_s, gq_r, grad = refs
        side_s, side_r, seen_by = (q_s, g_s, rows_s), ((q_r0, q_r1), (g_r0, g_r1), None), 1
    else:
        gq_r_in, gq_s_in, out, gq_r, gq_s, grad = refs
        side_s, side_r, seen_by = ((q_r0, q_r1), (g_r0, g_r1), None), (q_s, g_s, rows_s), 0
    device = lax.axis_index(AXIS)
    core = device % 2
    valid = device // 2 >= 2

    @pl.when(valid)
    def _():
        tile(kv, side_s, grad, gq_s_in, gq_s, W, True)

    @pl.when(valid & (core == seen_by))
    def _():
        tile(kv, side_r, grad, gq_r_in, gq_r, None, False)

    @pl.when(valid)
    def _():
        scale_keys(grad)
        out[...] = grad[...].astype(out.dtype)

    @pl.when(jnp.logical_not(valid))
    def _():
        out[...] = jnp.zeros_like(out)
        gq_s[...] = gq_s_in[...]

    @pl.when(jnp.logical_not(valid & (core == seen_by)))
    def _():
        gq_r[...] = gq_r_in[...]


def near_kernel(kv, q_s, g_s, rows_s, q_r0, q_r1, g_r0, g_r1, gq_s_in, gq_r_in, out, gq_s, gq_r, grad):
    side_s, side_r = (q_s, g_s, rows_s), ((q_r0, q_r1), (g_r0, g_r1), None)
    valid = lax.axis_index(AXIS) // 2 >= 1

    @pl.when(valid)
    def _():
        tile(kv, side_s, grad, gq_s_in, gq_s, None, True)
        tile(kv, side_r, grad, gq_r_in, gq_r, None, False)
        scale_keys(grad)
        out[...] = grad[...].astype(out.dtype)

    @pl.when(jnp.logical_not(valid))
    def _():
        out[...] = jnp.zeros_like(out)
        gq_s[...] = gq_s_in[...]
        gq_r[...] = gq_r_in[...]


def final_q_kernel(own_ref, got_ref, after, out_ref, token_ref, wide):
    token_ref[...] = jnp.zeros_like(token_ref)
    rows, heads, size = out_ref.shape
    half = heads // 2
    core = lax.axis_index(AXIS) % 2
    flat = wide.reshape(rows * heads, size)
    share = half // own_ref.shape[0]
    skip = got_ref.shape[0] - half
    for j in range(half):
        g, r = j // share, j % share
        flat[pl.ds(core * half + j, rows, stride=heads), :] = own_ref[g, r * rows : (r + 1) * rows] * query_scale
        flat[pl.ds((1 - core) * half + j, rows, stride=heads), :] = got_ref[skip + j].astype(jnp.float32)
    out_ref[...] = wide[...].astype(out_ref.dtype)


def partial_kernel(own_ref, back_ref, out_ref):
    out_ref[...] = own_ref[...] + back_ref[...].astype(jnp.float32)


def final_kv_kernel(part_ref, got_ref, back_r, side_s, side_r, after, out_k, out_v, wide):
    rows, heads, size = out_k.shape
    half = heads // 2
    core = lax.axis_index(AXIS) % 2
    flat = wide.reshape(rows * 2 * heads, size)
    for part in range(2):
        for j in range(half):
            n = part * half + j
            flat[pl.ds(part * heads + core * half + j, rows, stride=2 * heads), :] = part_ref[n] + side_s[n].astype(
                jnp.float32
            )
            flat[pl.ds(part * heads + (1 - core) * half + j, rows, stride=2 * heads), :] = (
                got_ref[n].astype(jnp.float32)
                + back_r[n].astype(jnp.float32)
                + side_r[n].astype(jnp.float32)
            )
    out_k[...] = wide[:, :heads, :].astype(out_k.dtype)
    out_v[...] = wide[:, heads:, :].astype(out_v.dtype)


def shards(queries, key_rows, value_rows, attn_output, grad_output, log_norm):
    rows, heads, size = queries.shape
    groups = key_rows.shape[1]
    devices = lax.axis_size(AXIS)
    hops = W // rows
    assert hops == 4 and devices % 4 == 0
    low, f32 = jnp.bfloat16, jnp.float32
    device = lax.axis_index(AXIS)
    even = (device // 2) % 2 == 0

    def move(x, target):
        pairs = [(i, target(i)) for i in range(devices)]
        return lax.ppermute(x, AXIS, [(i, j) for i, j in pairs if j >= 0])

    ahead = lambda i: (i + hops) % devices
    behind = lambda i: (i - hops) % devices
    sibling = lambda i: i ^ 1
    beside = lambda i: i ^ 2

    shape = jax.ShapeDtypeStruct
    kv_block = (groups, rows, size)
    half_rows = heads * rows // 2
    row_block = (heads * rows // size, size)
    gq_block = (groups // 2, heads // groups * rows, size)

    hbm = pl.BlockSpec(memory_space=pltpu.HBM)
    vmem = pl.BlockSpec(memory_space=pltpu.VMEM)
    anywhere = pl.BlockSpec(memory_space=pl.ANY)
    hbm = pl.BlockSpec(memory_space=pltpu.HBM)
    vmem = pl.BlockSpec(memory_space=pltpu.VMEM)
    anywhere = pl.BlockSpec(memory_space=pl.ANY)

    def pin(x):
        return pltpu.with_memory_space_constraint(x, pltpu.HBM)

    kv_s, kv_give = call(
        pack_kv_kernel,
        "pack_kv",
        [shape(kv_block, low)] * 2,
        [pltpu.VMEM(key_rows.shape, low)] * 2
        + [pltpu.VMEM((rows, 2 * groups, size), f32), pltpu.SemaphoreType.DMA((2,))],
        in_specs=[hbm, hbm],
    )(pin(key_rows), pin(value_rows))
    kv_r = move(kv_give, sibling)
    two_s = move(kv_s, ahead)
    two_r = move(kv_r, ahead)
    q_s, g_s, rows_s, *gives = call(
        pack_q_kernel,
        "pack_q",
        [
            shape((half_rows, size), low),
            shape((half_rows, size), low),
            shape(row_block, f32),
            shape((half_rows // 2 + 3 * row_block[0], size), low),
            shape((half_rows // 2, size), low),
            shape((half_rows // 2, size), low),
            shape((half_rows // 2, size), low),
        ],
        [pltpu.VMEM(queries.shape, low)] * 3
        + [pltpu.VMEM((rows, heads, size), f32), pltpu.VMEM(row_block, f32), pltpu.SemaphoreType.DMA((3,))],
        in_specs=[hbm, hbm, hbm, vmem, anywhere],
    )(pin(queries), pin(grad_output), pin(attn_output), log_norm, kv_r)
    received = [move(x, sibling) for x in gives]
    acc = [shape(gq_block, f32)] * 2
    grad_scratch = [pltpu.VMEM(kv_block, f32)]
    grad_s, gq_s = call(own_side_kernel, "own_side", [shape(kv_block, f32), acc[0]], flops=0)(
        kv_s, q_s, g_s, rows_s
    )
    sides = (q_s, g_s, rows_s, *received)
    own_s, own_r, gq_s, gq_r = call(own_rest_kernel, "own_rest", [shape(kv_block, f32)] * 2 + acc, flops=0)(
        kv_s, kv_r, *sides, grad_s, gq_s
    )
    two_s, gq_s, gq_r = lax.optimization_barrier((two_s, gq_s, gq_r))
    send_s = jnp.where(even, kv_s, two_s)
    one_s = move(send_s, beside)
    gq_s, gq_r, send_s = lax.optimization_barrier((gq_s, gq_r, send_s))
    far_s, gq_s, gq_r = call(
        functools.partial(far_kernel, True), "far_s", [shape(kv_block, low)] + acc, grad_scratch
    )(two_s, *sides, gq_s, gq_r)
    back_s = move(far_s, behind)
    two_r, gq_s, gq_r = lax.optimization_barrier((two_r, gq_s, gq_r))
    one_r = move(jnp.where(even, kv_r, two_r), beside)
    far_r, gq_s, gq_r = call(
        functools.partial(far_kernel, False),
        "far_r",
        [shape(kv_block, low)] + acc,
        grad_scratch,
    )(two_r, *sides, gq_s, gq_r)
    back_r = move(far_r, lambda i: sibling(behind(i)))
    near = functools.partial(call, near_kernel, out_shape=[shape(kv_block, low)] + acc, scratch=grad_scratch)
    near_s, gq_s, gq_r = near(name="near_s")(one_s, *sides, gq_s, gq_r)
    side_s = move(near_s, lambda i: i - 2)
    back_s, one_r = lax.optimization_barrier((back_s, one_r))
    near_r, gq_s, gq_r = near(name="near_r")(one_r, *sides, gq_s, gq_r)
    side_r = move(near_r, lambda i: sibling((i - 2) % devices))

    part = call(partial_kernel, "partial", shape(kv_block, f32), flops=LONG)(own_s, back_s)
    give = jnp.concatenate([own_r.astype(low), (gq_r * query_scale).astype(low).reshape(-1, rows, size)])
    got = move(give, sibling)
    grad_q, token = call(
        final_q_kernel,
        "final_q",
        [shape(queries.shape, low), shape((8, 128), f32)],
        [pltpu.VMEM((rows, heads, size), f32)],
        in_specs=[vmem, vmem, anywhere],
    )(gq_s, got, part)
    grad_k, grad_v = call(
        final_kv_kernel,
        "final_kv",
        [shape(key_rows.shape, low), shape(value_rows.shape, low)],
        [pltpu.VMEM((rows, 2 * groups, size), f32)],
        in_specs=[vmem] * 5 + [anywhere],
    )(part, got, back_r, side_s, side_r, token)
    return grad_q, grad_k, grad_v


def solution(mesh):
    in_specs = (
        P("seq", None, None),
        P("seq", None, None),
        P("seq", None, None),
        P("seq", None, None),
        P("seq", None, None),
        P(None, "seq"),
    )
    out_specs = (P("seq", None, None), P("seq", None, None), P("seq", None, None))
    return jax.shard_map(shards, mesh=mesh, in_specs=in_specs, out_specs=out_specs, check_vma=False)
```

```python
import functools
import math

import jax
import jax.numpy as jnp
from jax import lax
from jax.experimental import pallas as pl
from jax.experimental.pallas import tpu as pltpu
from jax.sharding import PartitionSpec as P

W = 1024

query_scale = 168.0 ** (-0.5)
LOG2E = math.log2(math.e)
AXIS = "seq"
VMEM_LIMIT = 16 * 1024 * 1024
LONG = 10**10
CHUNKS = 2

NT = (((1,), (1,)), ((), ()))
NN = (((1,), (0,)), ((), ()))
TN = (((0,), (0,)), ((), ()))


def dot(a, b, dims):
    return lax.dot_general(a, b, dims, preferred_element_type=jnp.float32)


def call(kernel, name, out_shape, scratch=(), flops=0, **specs):
    return pl.pallas_call(
        kernel,
        out_shape=out_shape,
        scratch_shapes=list(scratch),
        name=name,
        cost_estimate=pl.CostEstimate(flops=flops, bytes_accessed=2 << 20, transcendentals=0),
        compiler_params=pltpu.CompilerParams(vmem_limit_bytes=VMEM_LIMIT),
        **specs,
    )


def fetch(pairs, sems):
    copies = [pltpu.make_async_copy(src, dst, sems.at[n]) for n, (src, dst) in enumerate(pairs)]
    for copy in copies:
        copy.start()
    return copies


def pack_kv_kernel(k_hbm, v_hbm, keep_ref, give_ref, k_ref, v_ref, wide, sems):
    copy_k, copy_v = fetch(((k_hbm, k_ref), (v_hbm, v_ref)), sems)
    rows, heads, _ = k_ref.shape
    half = heads // 2
    core = lax.axis_index(AXIS) % 2
    copy_k.wait()
    wide[:, :heads, :] = k_ref[...].astype(jnp.float32)
    copy_v.wait()
    wide[:, heads:, :] = v_ref[...].astype(jnp.float32)
    flat = wide.reshape(rows * 2 * heads, wide.shape[2])
    for out, side in ((keep_ref, core), (give_ref, 1 - core)):
        for part in range(2):
            for j in range(half):
                head = part * heads + side * half + j
                out[part * half + j] = flat[pl.ds(head, rows, stride=2 * heads), :].astype(out.dtype)


def split_three(x):
    parts = []
    for _ in range(3):
        part = x.astype(jnp.bfloat16)
        parts.append(part)
        x = x - part.astype(jnp.float32)
    return parts


def join_three(ref, start, count):
    high, mid, low = (ref[start + n * count : start + (n + 1) * count].astype(jnp.float32) for n in range(3))
    return high + mid + low


def pack_q_kernel(
    q_hbm,
    g_hbm,
    o_hbm,
    norm_ref,
    after,
    keep_q,
    keep_g,
    keep_rows,
    give_q0,
    give_q1,
    give_g0,
    give_g1,
    q_ref,
    g_ref,
    o_ref,
    wide,
    give_rows,
    sems,
):
    copy_q, copy_g, copy_o = fetch(((q_hbm, q_ref), (g_hbm, g_ref), (o_hbm, o_ref)), sems)
    rows, heads, size = q_ref.shape
    half = heads // 2
    pieces = rows // size
    core = lax.axis_index(AXIS) % 2
    ones = jnp.ones((16, size), jnp.bfloat16)
    flat = wide.reshape(rows * heads, size)

    def spread(outs):
        keep, low, high = outs
        for j in range(half):
            block = flat[pl.ds(core * half + j, rows, stride=heads), :]
            keep[j * rows : (j + 1) * rows] = block.astype(keep.dtype)
            block = flat[pl.ds((1 - core) * half + j, rows, stride=heads), :]
            out, at = (low, j) if j < half // 2 else (high, j - half // 2)
            out[at * rows : (at + 1) * rows] = block.astype(out.dtype)

    copy_q.wait()
    wide[...] = q_ref[...].astype(jnp.float32)
    spread((keep_q, give_q0, give_q1))
    copy_g.wait()
    wide[...] = g_ref[...].astype(jnp.float32)
    spread((keep_g, give_g0, give_g1))
    copy_o.wait()
    wide[...] = g_ref[...].astype(jnp.float32) * o_ref[...].astype(jnp.float32)
    for out, side in ((keep_rows, core), (give_rows, 1 - core)):
        for j in range(half):
            product = flat[pl.ds(side * half + j, rows, stride=heads), :]
            high = product.astype(jnp.bfloat16)
            rest = (product - high.astype(jnp.float32)).astype(jnp.bfloat16)
            delta = dot(ones, high, NT) + dot(ones, rest, NT)
            norm = norm_ref[pl.ds(side * half + j, 1), :] * LOG2E
            for n in range(pieces):
                out[j * pieces + n : j * pieces + n + 1] = norm[:, n * size : (n + 1) * size]
                at = (half + j) * pieces + n
                out[at : at + 1] = delta[:1, n * size : (n + 1) * size]
    count = heads * pieces
    for n, part in enumerate(split_three(give_rows[...])):
        start = half // 2 * rows + n * count
        give_q0[start : start + count] = part


def tile(kv_ref, side, grad_ref, gq_in, gq_ref, offset, first):
    q_ref, g_ref, row_ref = side
    groups = kv_ref.shape[0] // 2
    rows, size = kv_ref.shape[1], kv_ref.shape[2]
    span = gq_ref.shape[1]
    share = span // rows
    pieces = span // size
    if row_ref is None:
        vectors = join_three(q_ref[0], g_ref[0].shape[0], 2 * groups * pieces)
    else:
        vectors = row_ref[...]

    def vector(at):
        return jnp.concatenate([vectors[at + n : at + n + 1] for n in range(pieces)], 1)

    for g in range(groups):
        k = kv_ref[g]
        v = kv_ref[groups + g]
        if row_ref is None:
            q, d = q_ref[g][:span], g_ref[g][...]
        else:
            q = q_ref[g * span : (g + 1) * span]
            d = g_ref[g * span : (g + 1) * span]
        norm = vector(g * pieces)
        delta = vector((groups + g) * pieces)
        x = dot(k, q, NT) * (query_scale * LOG2E) - norm
        if offset is not None:
            key = lax.broadcasted_iota(jnp.int32, (rows, rows), 0)
            query = lax.broadcasted_iota(jnp.int32, (rows, rows), 1)
            gap = query - key + offset
            seen = (gap >= 0) & (gap < W)
            x = jnp.concatenate(
                [jnp.where(seen, x[:, j * rows : (j + 1) * rows], -jnp.inf) for j in range(share)], 1
            )
        p = jnp.exp2(x)
        ds = (p * (dot(v, d, NT) - delta)).astype(jnp.bfloat16)
        gv = dot(p.astype(jnp.bfloat16), d, NN)
        gk = dot(ds, q, NN)
        gq = dot(ds, k, TN)
        if first:
            grad_ref[g] = gk
            grad_ref[groups + g] = gv
        else:
            grad_ref[g] += gk
            grad_ref[groups + g] += gv
        gq_ref[g] = gq if gq_in is None else gq_in[g] + gq


def scale_keys(grad_ref):
    groups = grad_ref.shape[0] // 2
    grad_ref[:groups] = grad_ref[:groups] * query_scale


def own_side_kernel(kv_s, q_s, g_s, rows_s, grad_s, gq_s):
    tile(kv_s, (q_s, g_s, rows_s), grad_s, None, gq_s, 0, True)


def own_rest_kernel(kv_s, kv_r, q_s, g_s, rows_s, q_r0, q_r1, g_r0, g_r1, grad_s_in, gq_s_in, grad_s, grad_r, gq_s, gq_r):
    side_s, side_r = (q_s, g_s, rows_s), ((q_r0, q_r1), (g_r0, g_r1), None)
    core = lax.axis_index(AXIS) % 2
    grad_s[...] = grad_s_in[...]
    tile(kv_r, side_r, grad_r, None, gq_r, 0, True)

    @pl.when(core == 0)
    def _():
        tile(kv_s, side_r, grad_s, gq_r, gq_r, None, False)
        gq_s[...] = gq_s_in[...]

    @pl.when(core == 1)
    def _():
        tile(kv_r, side_s, grad_r, gq_s_in, gq_s, None, False)

    scale_keys(grad_s)
    scale_keys(grad_r)


def far_kernel(first, kv, q_s, g_s, rows_s, q_r0, q_r1, g_r0, g_r1, *refs):
    if first:
        gq_s_in, gq_r_in, out, gq_s, gq_r, grad = refs
        side_s, side_r, seen_by = (q_s, g_s, rows_s), ((q_r0, q_r1), (g_r0, g_r1), None), 1
    else:
        gq_r_in, gq_s_in, out, gq_r, gq_s, grad = refs
        side_s, side_r, seen_by = ((q_r0, q_r1), (g_r0, g_r1), None), (q_s, g_s, rows_s), 0
    device = lax.axis_index(AXIS)
    core = device % 2
    valid = device // 2 >= 2

    @pl.when(valid)
    def _():
        tile(kv, side_s, grad, gq_s_in, gq_s, W, True)

    @pl.when(valid & (core == seen_by))
    def _():
        tile(kv, side_r, grad, gq_r_in, gq_r, None, False)

    @pl.when(valid)
    def _():
        scale_keys(grad)
        out[...] = grad[...].astype(out.dtype)

    @pl.when(jnp.logical_not(valid))
    def _():
        out[...] = jnp.zeros_like(out)
        gq_s[...] = gq_s_in[...]

    @pl.when(jnp.logical_not(valid & (core == seen_by)))
    def _():
        gq_r[...] = gq_r_in[...]


def near_kernel(kv, q_s, g_s, rows_s, q_r0, q_r1, g_r0, g_r1, gq_s_in, gq_r_in, out, gq_s, gq_r, grad):
    side_s, side_r = (q_s, g_s, rows_s), ((q_r0, q_r1), (g_r0, g_r1), None)
    valid = lax.axis_index(AXIS) // 2 >= 1

    @pl.when(valid)
    def _():
        tile(kv, side_s, grad, gq_s_in, gq_s, None, True)
        tile(kv, side_r, grad, gq_r_in, gq_r, None, False)
        scale_keys(grad)
        out[...] = grad[...].astype(out.dtype)

    @pl.when(jnp.logical_not(valid))
    def _():
        out[...] = jnp.zeros_like(out)
        gq_s[...] = gq_s_in[...]
        gq_r[...] = gq_r_in[...]


def final_q_kernel(own_ref, got_ref, after, out_ref, token_ref, wide):
    token_ref[...] = jnp.zeros_like(token_ref)
    rows, heads, size = out_ref.shape
    half = heads // 2
    core = lax.axis_index(AXIS) % 2
    flat = wide.reshape(rows * heads, size)
    share = half // own_ref.shape[0]
    skip = got_ref.shape[0] - half
    for j in range(half):
        g, r = j // share, j % share
        flat[pl.ds(core * half + j, rows, stride=heads), :] = own_ref[g, r * rows : (r + 1) * rows] * query_scale
        flat[pl.ds((1 - core) * half + j, rows, stride=heads), :] = got_ref[skip + j].astype(jnp.float32)
    out_ref[...] = wide[...].astype(out_ref.dtype)


def partial_kernel(own_ref, back_ref, out_ref):
    out_ref[...] = own_ref[...] + back_ref[...].astype(jnp.float32)


def final_kv_kernel(part_ref, got_ref, back_r, side_s, side_r, after, hbm_k, hbm_v, out_k, out_v, wide, sems):
    rows, heads, size = out_k.shape
    half = heads // 2
    core = lax.axis_index(AXIS) % 2
    flat = wide.reshape(rows * 2 * heads, size)
    chunk = rows // CHUNKS
    copies = []
    for c in range(CHUNKS):
        span = slice(c * chunk, (c + 1) * chunk)
        first = c * chunk * 2 * heads
        for part in range(2):
            for j in range(half):
                n = part * half + j
                own = part_ref[n, span] + side_s[n, span].astype(jnp.float32)
                flat[pl.ds(first + part * heads + core * half + j, chunk, stride=2 * heads), :] = own
                other = (
                    got_ref[n, span].astype(jnp.float32)
                    + back_r[n, span].astype(jnp.float32)
                    + side_r[n, span].astype(jnp.float32)
                )
                flat[pl.ds(first + part * heads + (1 - core) * half + j, chunk, stride=2 * heads), :] = other
        out_k[span] = wide[span, :heads, :].astype(out_k.dtype)
        out_v[span] = wide[span, heads:, :].astype(out_v.dtype)
        pairs = ((out_k.at[span], hbm_k.at[span]), (out_v.at[span], hbm_v.at[span]))
        copies += fetch(pairs, sems.at[c])
    for copy in copies:
        copy.wait()


def shards(queries, key_rows, value_rows, attn_output, grad_output, log_norm):
    rows, heads, size = queries.shape
    groups = key_rows.shape[1]
    devices = lax.axis_size(AXIS)
    hops = W // rows
    assert hops == 4 and devices % 4 == 0
    low, f32 = jnp.bfloat16, jnp.float32
    device = lax.axis_index(AXIS)
    even = (device // 2) % 2 == 0

    def move(x, target):
        pairs = [(i, target(i)) for i in range(devices)]
        return lax.ppermute(x, AXIS, [(i, j) for i, j in pairs if j >= 0])

    ahead = lambda i: (i + hops) % devices
    behind = lambda i: (i - hops) % devices
    sibling = lambda i: i ^ 1
    beside = lambda i: i ^ 2

    shape = jax.ShapeDtypeStruct
    kv_block = (groups, rows, size)
    half_rows = heads * rows // 2
    row_block = (heads * rows // size, size)
    gq_block = (groups // 2, heads // groups * rows, size)

    hbm = pl.BlockSpec(memory_space=pltpu.HBM)
    vmem = pl.BlockSpec(memory_space=pltpu.VMEM)
    anywhere = pl.BlockSpec(memory_space=pl.ANY)
    hbm = pl.BlockSpec(memory_space=pltpu.HBM)
    vmem = pl.BlockSpec(memory_space=pltpu.VMEM)
    anywhere = pl.BlockSpec(memory_space=pl.ANY)

    def pin(x):
        return pltpu.with_memory_space_constraint(x, pltpu.HBM)

    kv_s, kv_give = call(
        pack_kv_kernel,
        "pack_kv",
        [shape(kv_block, low)] * 2,
        [pltpu.VMEM(key_rows.shape, low)] * 2
        + [pltpu.VMEM((rows, 2 * groups, size), f32), pltpu.SemaphoreType.DMA((2,))],
        in_specs=[hbm, hbm],
    )(pin(key_rows), pin(value_rows))
    kv_r = move(kv_give, sibling)
    two_s = move(kv_s, ahead)
    two_r = move(kv_r, ahead)
    q_s, g_s, rows_s, *gives = call(
        pack_q_kernel,
        "pack_q",
        [
            shape((half_rows, size), low),
            shape((half_rows, size), low),
            shape(row_block, f32),
            shape((half_rows // 2 + 3 * row_block[0], size), low),
            shape((half_rows // 2, size), low),
            shape((half_rows // 2, size), low),
            shape((half_rows // 2, size), low),
        ],
        [pltpu.VMEM(queries.shape, low)] * 3
        + [pltpu.VMEM((rows, heads, size), f32), pltpu.VMEM(row_block, f32), pltpu.SemaphoreType.DMA((3,))],
        in_specs=[hbm, hbm, hbm, vmem, anywhere],
    )(pin(queries), pin(grad_output), pin(attn_output), log_norm, kv_r)
    received = [move(x, sibling) for x in gives]
    acc = [shape(gq_block, f32)] * 2
    grad_scratch = [pltpu.VMEM(kv_block, f32)]
    grad_s, gq_s = call(own_side_kernel, "own_side", [shape(kv_block, f32), acc[0]], flops=0)(
        kv_s, q_s, g_s, rows_s
    )
    sides = (q_s, g_s, rows_s, *received)
    own_s, own_r, gq_s, gq_r = call(own_rest_kernel, "own_rest", [shape(kv_block, f32)] * 2 + acc, flops=0)(
        kv_s, kv_r, *sides, grad_s, gq_s
    )
    two_s, gq_s, gq_r = lax.optimization_barrier((two_s, gq_s, gq_r))
    send_s = jnp.where(even, kv_s, two_s)
    one_s = move(send_s, beside)
    gq_s, gq_r, send_s = lax.optimization_barrier((gq_s, gq_r, send_s))
    far_s, gq_s, gq_r = call(
        functools.partial(far_kernel, True), "far_s", [shape(kv_block, low)] + acc, grad_scratch
    )(two_s, *sides, gq_s, gq_r)
    back_s = move(far_s, behind)
    two_r, gq_s, gq_r = lax.optimization_barrier((two_r, gq_s, gq_r))
    one_r = move(jnp.where(even, kv_r, two_r), beside)
    far_r, gq_s, gq_r = call(
        functools.partial(far_kernel, False),
        "far_r",
        [shape(kv_block, low)] + acc,
        grad_scratch,
    )(two_r, *sides, gq_s, gq_r)
    back_r = move(far_r, lambda i: sibling(behind(i)))
    near = functools.partial(call, near_kernel, out_shape=[shape(kv_block, low)] + acc, scratch=grad_scratch)
    near_s, gq_s, gq_r = near(name="near_s")(one_s, *sides, gq_s, gq_r)
    side_s = move(near_s, lambda i: i - 2)
    back_s, one_r = lax.optimization_barrier((back_s, one_r))
    near_r, gq_s, gq_r = near(name="near_r")(one_r, *sides, gq_s, gq_r)
    side_r = move(near_r, lambda i: sibling((i - 2) % devices))

    part = call(partial_kernel, "partial", shape(kv_block, f32), flops=LONG)(own_s, back_s)
    give = jnp.concatenate([own_r.astype(low), (gq_r * query_scale).astype(low).reshape(-1, rows, size)])
    got = move(give, sibling)
    grad_q, token = call(
        final_q_kernel,
        "final_q",
        [shape(queries.shape, low), shape((8, 128), f32)],
        [pltpu.VMEM((rows, heads, size), f32)],
        in_specs=[vmem, vmem, anywhere],
    )(gq_s, got, part)
    grad_k, grad_v = call(
        final_kv_kernel,
        "final_kv",
        [shape(key_rows.shape, low), shape(value_rows.shape, low)],
        [pltpu.VMEM(key_rows.shape, low)] * 2
        + [pltpu.VMEM((rows, 2 * groups, size), f32), pltpu.SemaphoreType.DMA((CHUNKS, 2))],
        in_specs=[vmem] * 5 + [anywhere],
        out_specs=[hbm, hbm],
    )(part, got, back_r, side_s, side_r, token)
    return grad_q, grad_k, grad_v


def solution(mesh):
    in_specs = (
        P("seq", None, None),
        P("seq", None, None),
        P("seq", None, None),
        P("seq", None, None),
        P("seq", None, None),
        P(None, "seq"),
    )
    out_specs = (P("seq", None, None), P("seq", None, None), P("seq", None, None))
    return jax.shard_map(shards, mesh=mesh, in_specs=in_specs, out_specs=out_specs, check_vma=False)
```
